512 devices in a mesh: seq: 16 (over z_lo, core), dp: 32 (over z_hi, x, y).
Axes of the slice: x: 4, y: 4, z: 16 (z_hi: 2, z_lo: 8; z = z_hi * 8 + z_lo), core: 2. Of those that a mesh axis runs over, the one named last changes fastest.
Arguments:
- frames: bfloat16 [32, 16, 512, 1152], P('dp', 'seq'), may hold values from -6 to 6
- shift_table: float32 [32, 1152], P('dp'), may hold values from -3 to 3
- scale_table: float32 [32, 1152], P('dp'), may hold values from -0.5 to 2
- grad_attended: bfloat16 [32, 16, 512, 576], P('dp', 'seq'), may hold values from -6 to 6
- w_qkv: bfloat16 [1152, 1728], P('seq'), may hold values from -0.1875 to 0.1875
Outputs:
- grad_frames: bfloat16 [32, 16, 512, 1152], P('dp', 'seq')
- grad_weight: bfloat16 [1152, 1728], P('seq')
The draws below stay inside these ranges and needn't reach their ends.
All inputs are finite; a program needn't handle non-finite values.
Results may differ from the reference program's by a relative error of at most 0.035.
Values may be sent and summed in bfloat16 or wider, within the bound.
A program may use at most 64 MiB of HBM per device.

```python
import jax
import jax.numpy as jnp
from jax import lax

D = 1152
HEADS = 8
HD = 72
PATCH = 512
FRAMES = 16
VIDEOS = 32


def draw_scale_table(key, part):
    key = jax.random.fold_in(key, 7)
    base = jax.random.uniform(jax.random.fold_in(key, 1), (VIDEOS, D), jnp.float32, -0.5, 0.5)
    return base


def levels(rng, dims, shards, smallest, largest):
    factor_of, own = 1.0, jax.random.fold_in(rng, 6)
    for dim, parts in shards:
        heights = jnp.exp(jax.random.uniform(jax.random.fold_in(own, dim), (parts,), jnp.float32, smallest / len(shards), largest / len(shards)))
        factor_of = factor_of * jnp.repeat(heights, dims[dim] // parts).reshape([-1 if axis == dim else 1 for axis in range(len(dims))])
    return factor_of


def gaussian(stream_key, shape, width, most, cuts=(), dtype=jnp.bfloat16):
    drawn = width * jax.random.normal(stream_key, shape, jnp.float32)
    if cuts:
        drawn = drawn * levels(stream_key, shape, cuts, -0.22, 0.18)
    return jnp.clip(drawn, -most, most).astype(dtype)


def setup_inputs(seed: int = 0) -> dict:
    key_of = jax.random.split(jax.random.key(seed), 6)
    return {
        "frames": gaussian(key_of[0], (VIDEOS, FRAMES, PATCH, D), 1.0, 6.0, ((0, 32), (1, 16))),
        "shift_table": gaussian(key_of[1], (VIDEOS, D), 0.5, 3.0, ((0, 32),), jnp.float32),
        "scale_table": draw_scale_table(jax.random.fold_in(key_of[5], 71), 0),
        "grad_attended": gaussian(key_of[3], (VIDEOS, FRAMES, PATCH, HEADS * HD), 1.0, 6.0, ((0, 32), (1, 16))),
        "w_qkv": gaussian(key_of[4], (D, 3 * HEADS * HD), D ** -0.5, 0.1875, ((0, 16),)),
    }


epsilon = 1e-06

def modulate(tokens, shift_row, scale_row):
    values = tokens.astype(jnp.float32)
    centre = lax.optimization_barrier(jnp.mean(values, axis=-1, keepdims=True))
    centred = values - centre
    spread = lax.optimization_barrier(jnp.mean(centred * centred, axis=-1, keepdims=True))
    return centred * lax.rsqrt(spread + epsilon) * (1.0 + scale_row) + shift_row

def attention_backward(projected, cotangent):
    frame_n, patch_n, columns = projected.shape
    inner = columns // 3
    head_n = inner // HD
    factor = HD ** (-0.5)
    query = projected[:, :, :inner].astype(jnp.float32).reshape(frame_n, patch_n, head_n, HD)
    key_rows = projected[:, :, inner:2 * inner].astype(jnp.float32).reshape(frame_n, patch_n, head_n, HD)
    value_rows = projected[:, :, 2 * inner:].astype(jnp.float32).reshape(frame_n, patch_n, head_n, HD)
    grad_out = cotangent.astype(jnp.float32).reshape(frame_n, patch_n, head_n, HD)
    scores = jnp.einsum('fphd,gphd->phfg', query, key_rows) * factor
    highest = lax.optimization_barrier(jnp.max(scores, axis=-1, keepdims=True))
    expo = jnp.exp(scores - highest)
    attend = expo / lax.optimization_barrier(jnp.sum(expo, axis=-1, keepdims=True))
    attend_b = attend.astype(jnp.bfloat16).astype(jnp.float32)
    grad_value = jnp.einsum('phfg,fphd->gphd', attend_b, grad_out)
    dots = jnp.einsum('fphd,gphd->phfg', grad_out, value_rows)
    grad_scores = attend * (dots - lax.optimization_barrier(jnp.sum(attend * dots, axis=-1, keepdims=True))) * factor
    grad_scores = grad_scores.astype(jnp.bfloat16).astype(jnp.float32)
    grad_query = jnp.einsum('phfg,gphd->fphd', grad_scores, key_rows)
    grad_key = jnp.einsum('phfg,fphd->gphd', grad_scores, query)
    joined = jnp.concatenate([grad_query.reshape(frame_n, patch_n, inner), grad_key.reshape(frame_n, patch_n, inner), grad_value.reshape(frame_n, patch_n, inner)], axis=-1)
    return joined.astype(jnp.bfloat16)

def reference(frames, shift_table, scale_table, grad_attended, w_qkv):
    columns = 3 * HEADS * HD

    def per_video(total, items):
        tokens, shift_row, scale_row, cotangent = items
        normed = modulate(tokens, shift_row, scale_row).astype(jnp.bfloat16)
        token_rows = normed.reshape(-1, D)
        projected = jnp.dot(token_rows, w_qkv, preferred_element_type=jnp.float32).astype(jnp.bfloat16)
        projected = projected.reshape(FRAMES, PATCH, columns)
        grad_projected = attention_backward(projected, cotangent)
        grad_rows = grad_projected.reshape(-1, columns)
        grad_normed = lax.dot_general(grad_rows, w_qkv, (((1,), (1,)), ((), ())), preferred_element_type=jnp.float32)
        unused, pull = jax.vjp(lambda inner_tokens: modulate(inner_tokens, shift_row, scale_row), tokens)
        grad_tokens = pull(grad_normed.reshape(tokens.shape))[0]
        left = token_rows.astype(jnp.float32).reshape(FRAMES, PATCH, D)
        right = grad_rows.astype(jnp.float32).reshape(FRAMES, PATCH, columns)
        partial_sums = jnp.einsum('fpd,fpe->fde', left, right).astype(jnp.bfloat16)
        partial_sums = lax.optimization_barrier(partial_sums).astype(jnp.float32)
        return (total + lax.optimization_barrier(jnp.sum(partial_sums, axis=0)), grad_tokens)
    start_total = jnp.zeros((D, columns), jnp.float32)
    total, grad_frames = lax.scan(per_video, start_total, (frames, shift_table, scale_table, grad_attended))
    return (grad_frames, total.astype(jnp.bfloat16))
```

```python
import functools

import jax
import jax.numpy as jnp
from jax import lax
from jax.experimental import pallas as pl
from jax.experimental.pallas import tpu as pltpu
from jax.sharding import PartitionSpec as P

MESH = pl.DeviceIdType.MESH
F32 = jnp.float32
BF16 = jnp.bfloat16

D = 1152
HD = 72
INNER = 576
WIDE = 640
SEQ = 16
NZ = 8
NXY = 16
NQ = 16
ROWS = 72
PATCH = 512
OWN = 32
CH = 2
CP = 16
TOK = SEQ * CP
epsilon = 1e-06


def place():
    s, d = lax.axis_index("seq"), lax.axis_index("dp")
    return s, d, lax.div(s, 2), lax.rem(s, 2), lax.div(d, NXY), lax.rem(d, NXY)


def remote(src, dst, send, recv, seq, dp):
    return pltpu.make_async_remote_copy(
        src_ref=src,
        dst_ref=dst,
        send_sem=send,
        recv_sem=recv,
        device_id={"seq": seq, "dp": dp},
        device_id_type=MESH,
    )


def loop(start, stop, body):
    def step(i, carry):
        body(i)
        return carry

    lax.fori_loop(start, stop, step, 0)


def greet(seq, dp):
    pl.semaphore_signal(
        pltpu.get_barrier_semaphore(),
        inc=1,
        device_id={"seq": seq, "dp": dp},
        device_id_type=MESH,
    )


def gather_kernel(wp, w_out, g1, g2, g3, s1, r1, s2, r2, s3, r3, own_sem):
    s, d, z, c, hi, q = place()
    base = hi * NXY
    sibling = 2 * z + 1 - c
    loop(1, NZ, lambda i: greet(2 * lax.rem(z + i, NZ) + c, d))
    loop(1, NXY, lambda i: greet(s, base + lax.rem(q + i, NXY)))
    greet(sibling, d)
    pl.semaphore_wait(pltpu.get_barrier_semaphore(), NZ - 1 + NXY - 1 + 1)

    def along_z(i):
        return remote(wp.at[q], g1.at[z], s1.at[i - 1], r1.at[i - 1], 2 * lax.rem(z + i, NZ) + c, d)

    loop(1, NZ, lambda i: along_z(i).start())
    own = pltpu.make_async_copy(wp.at[q], g1.at[z], own_sem)
    own.start()
    own.wait()
    loop(1, NZ, lambda i: along_z(i).wait_recv())

    def over_plane(i):
        return remote(g1, g2.at[q], s2.at[i - 1], r2.at[i - 1], s, base + lax.rem(q + i, NXY))

    loop(1, NXY, lambda i: over_plane(i).start())
    own = pltpu.make_async_copy(g1, g2.at[q], own_sem)
    own.start()
    own.wait()

    def across(i):
        piece = lax.rem(q + NXY - i, NXY)
        return remote(g2.at[piece], g3.at[piece], s3.at[i], r3.at[i], sibling, d)

    across(0).start()

    def pass_on(i):
        over_plane(i).wait_recv()
        across(i).start()

    loop(1, NXY, pass_on)
    loop(0, NXY, lambda i: across(i).wait_recv())

    def assemble(t):
        piece, row = lax.div(t, NZ), lax.rem(t, NZ)
        part, tile = lax.div(piece, 5), lax.rem(piece, 5)
        here = g2[piece, row].astype(F32)
        there = g3[piece, row].astype(F32)
        both = jnp.concatenate([jnp.where(c == 0, here, there), jnp.where(c == 0, there, here)], axis=0)
        w_out[part, pl.ds(pl.multiple_of(row * 144, 16), 144), pl.ds(pl.multiple_of(tile * 128, 128), 128)] = (
            both.astype(BF16)
        )

    loop(0, 15 * NZ, assemble)
    loop(1, NZ, lambda i: along_z(i).wait_send())
    loop(1, NXY, lambda i: over_plane(i).wait_send())
    loop(0, NXY, lambda i: across(i).wait_send())


def gather(wp):
    return pl.pallas_call(
        gather_kernel,
        out_shape=jax.ShapeDtypeStruct((3, D, WIDE), BF16),
        in_specs=[pl.BlockSpec(memory_space=pltpu.VMEM)],
        out_specs=pl.BlockSpec(memory_space=pltpu.VMEM),
        scratch_shapes=[
            pltpu.VMEM((NZ, ROWS, 128), BF16),
            pltpu.VMEM((NQ, NZ, ROWS, 128), BF16),
            pltpu.VMEM((NQ, NZ, ROWS, 128), BF16),
            pltpu.SemaphoreType.DMA((NZ - 1,)),
            pltpu.SemaphoreType.DMA((NZ - 1,)),
            pltpu.SemaphoreType.DMA((NXY - 1,)),
            pltpu.SemaphoreType.DMA((NXY - 1,)),
            pltpu.SemaphoreType.DMA((NXY,)),
            pltpu.SemaphoreType.DMA((NXY,)),
            pltpu.SemaphoreType.DMA,
        ],
        compiler_params=pltpu.CompilerParams(
            collective_id=0, has_side_effects=True, vmem_limit_bytes=48 * 1024 * 1024
        ),
        name="gather_weight",
    )(wp)


def dot_last(a, b):
    return lax.dot_general(a, b, (((1,), (1,)), ((), ())), preferred_element_type=F32)


def dot_first(a, b):
    return lax.dot_general(a, b, (((0,), (0,)), ((), ())), preferred_element_type=F32)


def centred_of(tokens):
    values = tokens.astype(F32)
    centred = values - jnp.mean(values, axis=-1, keepdims=True)
    spread = jnp.mean(centred * centred, axis=-1, keepdims=True)
    return centred, lax.rsqrt(spread + epsilon)


def chunk_backward(ch, tokens, cots, shift, scale, w, away, proj, gproj, normed, cot, acc, gnorm, block):
    first = pl.multiple_of(ch * TOK, TOK)
    rows = pl.ds(first, TOK)
    gain = 1.0 + scale[...]

    def norm(f):
        centred, rate = centred_of(tokens[ch, f])
        normed[pl.ds(pl.multiple_of(first + f * CP, CP), CP), :] = (centred * rate * gain + shift[...]).astype(BF16)
        cot[pl.ds(pl.multiple_of(f * CP, CP), CP), :] = cots[ch, f]

    loop(0, SEQ, norm)

    def project(i):
        proj[i] = jnp.dot(normed[rows, :], w[i], preferred_element_type=F32).astype(BF16)
        acc[i] = jnp.zeros((TOK, WIDE), F32)

    loop(0, 3, project)
    factor = HD ** (-0.5)

    def heads(a):
        lanes = pl.ds(pl.multiple_of(a * 128, 128), 256)
        query, key, value, grad = proj[0, :, lanes], proj[1, :, lanes], proj[2, :, lanes], cot[:, lanes]
        lane = lax.broadcasted_iota(jnp.int32, (TOK, 256), 1)
        for t in range(2):
            low = 16 * a + HD * t
            mask = jnp.where((lane >= low) & (lane < low + HD), 1.0, 0.0).astype(BF16)
            query_h, key_h, grad_h = query * mask, key * mask, grad * mask
            scores = dot_last(query_h, key) * factor + block[...]
            expo = jnp.exp(scores - jnp.max(scores, axis=-1, keepdims=True))
            attend = expo / jnp.sum(expo, axis=-1, keepdims=True)
            acc[2, :, lanes] += dot_first(attend.astype(BF16), grad_h)
            dots = dot_last(grad_h, value)
            gscores = attend * (dots - jnp.sum(attend * dots, axis=-1, keepdims=True)) * factor
            gscores = gscores.astype(BF16)
            acc[0, :, lanes] += jnp.dot(gscores, key_h, preferred_element_type=F32)
            acc[1, :, lanes] += dot_first(gscores, query_h)

    loop(0, 4, heads)

    def rounded(i):
        gproj[i, rows, :] = acc[i].astype(BF16)

    loop(0, 3, rounded)

    def grad_normed(n):
        part = pl.ds(pl.multiple_of(n * 384, 128), 384)
        total = dot_last(gproj[0, rows, :], w[0, part, :])
        total += dot_last(gproj[1, rows, :], w[1, part, :])
        total += dot_last(gproj[2, rows, :], w[2, part, :])
        gnorm[:, part] = total

    loop(0, 3, grad_normed)

    def grad_tokens(f):
        centred, rate = centred_of(tokens[ch, f])
        unit = centred * rate
        grad = gnorm[pl.ds(pl.multiple_of(f * CP, CP), CP), :] * gain
        mean = jnp.mean(grad, axis=-1, keepdims=True)
        along = jnp.mean(grad * unit, axis=-1, keepdims=True)
        away[ch, f] = (rate * (grad - mean - unit * along)).astype(BF16)

    loop(0, SEQ, grad_tokens)


def weight_partial(normed, gproj, gw):
    def part(t):
        i, n = lax.div(t, 3), lax.rem(t, 3)
        cut = pl.ds(pl.multiple_of(n * 384, 128), 384)
        gw[i, cut, :] = dot_first(normed[:, cut], gproj[i])

    loop(0, 9, part)


def main_kernel(
    x, cot_in, shift, scale, w, out, gw,
    tokens, cots, away, proj, gproj, normed, cot, acc, gnorm, block,
    sx, rx, sc, rc, sb, rb, own_sems,
):
    s, d, z, c, hi, q = place()
    loop(1, SEQ, lambda i: greet(lax.rem(s + i, SEQ), d))
    pl.semaphore_wait(pltpu.get_barrier_semaphore(), SEQ - 1)

    def rows_of(j, ch):
        return pl.ds(pl.multiple_of(j * OWN + ch * CP, CP), CP)

    def send_x(ch, i):
        j = lax.rem(s + i, SEQ)
        return remote(x.at[rows_of(j, ch)], tokens.at[ch, s], sx.at[ch, i - 1], rx.at[ch, i - 1], j, d)

    def send_c(ch, i):
        j = lax.rem(s + i, SEQ)
        return remote(cot_in.at[rows_of(j, ch)], cots.at[ch, s], sc.at[ch, i - 1], rc.at[ch, i - 1], j, d)

    def send_back(ch, i):
        j = lax.rem(s + i, SEQ)
        return remote(away.at[ch, j], out.at[rows_of(s, ch)], sb.at[ch, i - 1], rb.at[ch, i - 1], j, d)

    for ch in range(CH):

        def both(i):
            send_x(ch, i).start()
            send_c(ch, i).start()

        loop(1, SEQ, both)
    keeps = []
    for ch in range(CH):
        keeps.append(pltpu.make_async_copy(x.at[rows_of(s, ch)], tokens.at[ch, s], own_sems.at[ch]))
        keeps.append(pltpu.make_async_copy(cot_in.at[rows_of(s, ch)], cots.at[ch, s], own_sems.at[CH + ch]))
    for keep in keeps:
        keep.start()
    row = lax.broadcasted_iota(jnp.int32, (TOK, TOK), 0)
    column = lax.broadcasted_iota(jnp.int32, (TOK, TOK), 1)
    block[...] = jnp.where(lax.rem(row, CP) == lax.rem(column, CP), 0.0, -1e30)
    for keep in keeps:
        keep.wait()

    def chunk(ch):
        def arrived(i):
            send_x(ch, i).wait_recv()
            send_c(ch, i).wait_recv()

        loop(1, SEQ, arrived)
        chunk_backward(ch, tokens, cots, shift, scale, w, away, proj, gproj, normed, cot, acc, gnorm, block)
        loop(1, SEQ, lambda i: send_back(ch, i).start())
        mine = pltpu.make_async_copy(away.at[ch, s], out.at[rows_of(s, ch)], own_sems.at[0])
        mine.start()
        mine.wait()

    loop(0, CH, chunk)
    weight_partial(normed, gproj, gw)

    def finish(ch):
        def ends(i):
            send_x(ch, i).wait_send()
            send_c(ch, i).wait_send()
            send_back(ch, i).wait()

        loop(1, SEQ, ends)

    loop(0, CH, finish)


def main(x, cot, shift, scale, w):
    vm = pl.BlockSpec(memory_space=pltpu.VMEM)
    dma = pltpu.SemaphoreType.DMA
    return pl.pallas_call(
        main_kernel,
        out_shape=(jax.ShapeDtypeStruct((PATCH, D), BF16), jax.ShapeDtypeStruct((3, D, WIDE), F32)),
        in_specs=[vm] * 5,
        out_specs=(vm, vm),
        scratch_shapes=[
            pltpu.VMEM((CH, SEQ, CP, D), BF16),
            pltpu.VMEM((CH, SEQ, CP, WIDE), BF16),
            pltpu.VMEM((CH, SEQ, CP, D), BF16),
            pltpu.VMEM((3, TOK, WIDE), BF16),
            pltpu.VMEM((3, CH * TOK, WIDE), BF16),
            pltpu.VMEM((CH * TOK, D), BF16),
            pltpu.VMEM((TOK, WIDE), BF16),
            pltpu.VMEM((3, TOK, WIDE), F32),
            pltpu.VMEM((TOK, D), F32),
            pltpu.VMEM((TOK, TOK), F32),
            dma((CH, SEQ - 1)),
            dma((CH, SEQ - 1)),
            dma((CH, SEQ - 1)),
            dma((CH, SEQ - 1)),
            dma((CH, SEQ - 1)),
            dma((CH, SEQ - 1)),
            dma((2 * CH,)),
        ],
        compiler_params=pltpu.CompilerParams(
            collective_id=1, has_side_effects=True, vmem_limit_bytes=56 * 1024 * 1024
        ),
        name="attention_backward",
    )(x, cot, shift, scale, w)


def reduce_kernel(gw, out, away, near, half, plane, line, column, s0, r0, s1, r1, s2, r2, s3, r3):
    s, d, z, c, hi, q = place()
    base = hi * NXY
    sibling = 2 * z + 1 - c
    greet(sibling, d)
    loop(1, NXY, lambda i: greet(s, base + lax.rem(q + i, NXY)))

    def on_line(i):
        t = lax.rem(hi * NZ + z + i, 2 * NZ)
        return 2 * lax.rem(t, NZ) + c, lax.div(t, NZ) * NXY + q

    loop(1, 2 * NZ, lambda i: greet(*on_line(i)))
    pl.semaphore_wait(pltpu.get_barrier_semaphore(), 1 + NXY - 1 + 2 * NZ - 1)

    def block(piece, row, core):
        part, tile = lax.div(piece, 5), lax.rem(piece, 5)
        first = pl.multiple_of(row * 144 + core * ROWS, 8)
        return gw[part, pl.ds(first, ROWS), pl.ds(pl.multiple_of(tile * 128, 128), 128)]

    def across(i):
        piece = lax.rem(q + i, NXY)
        return remote(away.at[piece], near.at[piece], s0.at[i], r0.at[i], sibling, d)

    def give(i):
        piece = lax.rem(q + i, NXY)
        source = jnp.minimum(piece, 14)

        def rows(row):
            away[piece, row] = block(source, row, 1 - c).astype(BF16)

        loop(0, NZ, rows)
        across(i).start()

    loop(0, NXY, give)

    def over_plane(i):
        peer = lax.rem(q + i, NXY)
        return remote(half.at[peer], plane.at[i - 1], s1.at[i - 1], r1.at[i - 1], s, base + peer)

    def add_core(i):
        piece = lax.rem(q + i, NXY)
        source = jnp.minimum(piece, 14)
        across(i).wait_recv()

        def rows(row):
            half[piece, row] = (block(source, row, c) + near[piece, row].astype(F32)).astype(BF16)

        loop(0, NZ, rows)

    def add_and_send(i):
        add_core(i)
        over_plane(i).start()

    loop(1, NXY, add_and_send)
    add_core(0)
    loop(1, NXY, lambda i: over_plane(i).wait_recv())

    def add_plane(row):
        total = half[q, row].astype(F32)
        for i in range(1, NXY):
            total += plane[i - 1, row].astype(F32)
        line[row] = total.astype(BF16)

    loop(0, NZ, add_plane)

    def along(i):
        t = lax.rem(hi * NZ + z + i, 2 * NZ)
        seq, dp = on_line(i)
        return remote(line.at[lax.rem(t, NZ)], column.at[i - 1], s2.at[i - 1], r2.at[i - 1], seq, dp)

    loop(1, 2 * NZ, lambda i: along(i).start())
    loop(1, 2 * NZ, lambda i: along(i).wait_recv())
    total = line[z].astype(F32)
    for i in range(1, 2 * NZ):
        total += column[i - 1].astype(F32)
    out[q] = total.astype(BF16)

    def spread(i):
        return remote(out.at[q], out.at[q], s3.at[i - 1], r3.at[i - 1], s, base + lax.rem(q + i, NXY))

    loop(1, NXY, lambda i: spread(i).start())
    loop(1, NXY, lambda i: spread(i).wait())
    loop(0, NXY, lambda i: across(i).wait_send())
    loop(1, NXY, lambda i: over_plane(i).wait_send())
    loop(1, 2 * NZ, lambda i: along(i).wait_send())


def reduce_weight(gw):
    dma = pltpu.SemaphoreType.DMA
    return pl.pallas_call(
        reduce_kernel,
        out_shape=jax.ShapeDtypeStruct((NQ, ROWS, 128), BF16),
        in_specs=[pl.BlockSpec(memory_space=pltpu.VMEM)],
        out_specs=pl.BlockSpec(memory_space=pltpu.VMEM),
        scratch_shapes=[
            pltpu.VMEM((NQ, NZ, ROWS, 128), BF16),
            pltpu.VMEM((NQ, NZ, ROWS, 128), BF16),
            pltpu.VMEM((NQ, NZ, ROWS, 128), BF16),
            pltpu.VMEM((NXY - 1, NZ, ROWS, 128), BF16),
            pltpu.VMEM((NZ, ROWS, 128), BF16),
            pltpu.VMEM((2 * NZ - 1, ROWS, 128), BF16),
            dma((NXY,)),
            dma((NXY,)),
            dma((NXY - 1,)),
            dma((NXY - 1,)),
            dma((2 * NZ - 1,)),
            dma((2 * NZ - 1,)),
            dma((NXY - 1,)),
            dma((NXY - 1,)),
        ],
        compiler_params=pltpu.CompilerParams(
            collective_id=2, has_side_effects=True, vmem_limit_bytes=48 * 1024 * 1024
        ),
        name="reduce_weight",
    )(gw)


def body(frames, shift_table, scale_table, grad_attended, w_qkv):
    wide = jnp.pad(w_qkv.reshape(ROWS, 3, INNER), ((0, 0), (0, 0), (0, WIDE - INNER)))
    wide = jnp.pad(wide.reshape(ROWS, 15, 128), ((0, 0), (0, 1), (0, 0)))
    full = gather(wide.transpose(1, 0, 2))
    cot = jnp.pad(grad_attended[0, 0], ((0, 0), (0, WIDE - INNER)))
    grad_tokens, gw = main(frames[0, 0], cot, shift_table, scale_table, full)
    total = reduce_weight(gw)
    total = total[:15].transpose(1, 0, 2).reshape(ROWS, 3, WIDE)[:, :, :INNER]
    return grad_tokens[None, None], total.reshape(ROWS, 3 * INNER)


def solution(mesh):
    placed = (
        P("dp", "seq", None, None),
        P("dp", None),
        P("dp", None),
        P("dp", "seq", None, None),
        P("seq", None),
    )
    return jax.shard_map(
        body,
        mesh=mesh,
        in_specs=placed,
        out_specs=(P("dp", "seq", None, None), P("seq", None)),
        check_vma=False,
    )
```

```python
import jax
import jax.numpy as jnp
from jax import lax
from jax.experimental import pallas as pl
from jax.experimental.pallas import tpu as pltpu
from jax.sharding import PartitionSpec as P

MESH = pl.DeviceIdType.MESH
F32 = jnp.float32
BF16 = jnp.bfloat16

D = 1152
HD = 72
INNER = 576
WIDE = 640
SEQ = 16
NZ = 8
NXY = 16
NQ = 16
ROWS = 72
PATCH = 512
OWN = 32
CH = 2
CP = 16
TOK = SEQ * CP
epsilon = 1e-06


def place():
    s, d = lax.axis_index("seq"), lax.axis_index("dp")
    return s, d, lax.div(s, 2), lax.rem(s, 2), lax.div(d, NXY), lax.rem(d, NXY)


def remote(src, dst, send, recv, seq, dp):
    return pltpu.make_async_remote_copy(
        src_ref=src,
        dst_ref=dst,
        send_sem=send,
        recv_sem=recv,
        device_id={"seq": seq, "dp": dp},
        device_id_type=MESH,
    )


def loop(start, stop, body):
    def step(i, carry):
        body(i)
        return carry

    lax.fori_loop(start, stop, step, 0)


def greet(seq, dp):
    pl.semaphore_signal(
        pltpu.get_barrier_semaphore(),
        inc=1,
        device_id={"seq": seq, "dp": dp},
        device_id_type=MESH,
    )


def neighbours(me):
    return lax.rem(me + 1, 4), lax.rem(me + 3, 4), lax.rem(me + 2, 4)


def plane_device(h, stage, step, hi, x, y):
    along_x = (h == 0) == (stage == 0)
    me = x if along_x else y
    to = neighbours(me)[step]
    return hi * NXY + (to * 4 + y if along_x else x * 4 + to)


class Gather:
    def __init__(self, refs, spot):
        self.wp, self.w, self.g1, self.g2, self.g3, self.zs, self.zr, self.ps, self.pr, self.cs, self.cr, self.own = refs
        self.spot = spot

    def along_z(self, i):
        s, d, z, c, hi, q = self.spot
        return remote(
            self.wp.at[q], self.g1.at[z], self.zs.at[i - 1], self.zr.at[i - 1], 2 * lax.rem(z + i, NZ) + c, d
        )

    def plane(self, h, step, way):
        s, d, z, c, hi, q = self.spot
        x, y = lax.div(q, 4), lax.rem(q, 4)
        stage, passes = step // 2, step % 2
        low = 4 * h
        rows = pl.ds(low, 4)
        axis_x = (h == 0) == (stage == 0)
        other = neighbours(x if axis_x else y)[1 - way]
        if passes:
            rows = pl.ds(low + 2 * way, 2)
        if stage == 0:
            px, py = x, y
            if passes:
                px, py = (other, y) if axis_x else (x, other)
            piece = self.g2.at[px, py, rows]
        else:
            line = other if passes else (x if axis_x else y)
            piece = self.g2.at[line, :, rows] if axis_x else self.g2.at[:, line, rows]
        to = plane_device(h, stage, way, hi, x, y)
        return remote(piece, piece, self.ps.at[h, step, way], self.pr.at[h, step, way], s, to)

    def across(self, h, k):
        s, d, z, c, hi, q = self.spot
        x, y = lax.div(q, 4), lax.rem(q, 4)
        stage, which = k // 3, k % 3
        rows = pl.ds(4 * h, 4)
        axis_x = (h == 0) == (stage == 0)
        other = neighbours(x if axis_x else y)[which]

        def region(ref):
            if stage == 0:
                return ref.at[other, y, rows] if axis_x else ref.at[x, other, rows]
            return ref.at[other, :, rows] if axis_x else ref.at[:, other, rows]

        return remote(
            region(self.g2), region(self.g3), self.cs.at[h, k], self.cr.at[h, k], 2 * z + 1 - c, d
        )

    def own_across(self):
        s, d, z, c, hi, q = self.spot
        x, y = lax.div(q, 4), lax.rem(q, 4)
        return remote(self.g2.at[x, y], self.g3.at[x, y], self.cs.at[0, 6], self.cr.at[0, 6], 2 * z + 1 - c, d)

    def begin(self):
        loop(1, NZ, lambda i: self.along_z(i).start())

    def collect(self, between):
        s, d, z, c, hi, q = self.spot
        x, y = lax.div(q, 4), lax.rem(q, 4)
        own = pltpu.make_async_copy(self.wp.at[q], self.g1.at[z], self.own)
        own.start()
        own.wait()
        loop(1, NZ, lambda i: self.along_z(i).wait_recv())
        own = pltpu.make_async_copy(self.g1, self.g2.at[x, y], self.own)
        own.start()
        own.wait()
        for step in range(4):
            for h in range(2):
                if step:
                    for way in range(2):
                        self.plane(h, step - 1, way).wait_recv()
                for way in range(2):
                    self.plane(h, step, way).start()
                if step == 0 and h == 0:
                    self.own_across().start()
                if step % 2:
                    for k in range(2):
                        self.across(h, 3 * (step // 2) + k).start()
                elif step:
                    self.across(h, 2).start()
            between(step)
        for h in range(2):
            for way in range(2):
                self.plane(h, 3, way).wait_recv()
            self.across(h, 5).start()
        self.own_across().wait_recv()
        for h in range(2):
            for k in range(6):
                self.across(h, k).wait_recv()

        def assemble(t):
            piece, row = lax.div(t, NZ), lax.rem(t, NZ)
            part, tile = lax.div(piece, 5), lax.rem(piece, 5)
            px, py = lax.div(piece, 4), lax.rem(piece, 4)
            here = self.g2[px, py, row].astype(F32)
            there = self.g3[px, py, row].astype(F32)
            both = jnp.concatenate([jnp.where(c == 0, here, there), jnp.where(c == 0, there, here)], axis=0)
            lanes = pl.ds(pl.multiple_of(tile * 128, 128), 128)
            self.w[part, pl.ds(pl.multiple_of(row * 144, 16), 144), lanes] = both.astype(BF16)

        loop(0, 15 * NZ, assemble)

    def finish(self):
        loop(1, NZ, lambda i: self.along_z(i).wait_send())
        self.own_across().wait_send()
        for h in range(2):
            for step in range(4):
                for way in range(2):
                    self.plane(h, step, way).wait_send()
            for k in range(6):
                self.across(h, k).wait_send()


class Reduce:
    def __init__(self, refs, spot):
        (self.gw, self.out, self.away, self.near, self.half, self.a1, self.a2, self.b1, self.b2, self.column) = refs[:10]
        (self.cs, self.cr, self.ps, self.pr, self.zs, self.zr, self.ss, self.sr) = refs[10:]
        self.spot = spot

    def block(self, piece, row, core):
        part, tile = lax.div(piece, 5), lax.rem(piece, 5)
        first = pl.multiple_of(row * 144 + core * ROWS, 8)
        return self.gw[part, pl.ds(first, ROWS), pl.ds(pl.multiple_of(tile * 128, 128), 128)]

    def across(self, piece):
        s, d, z, c, hi, q = self.spot
        px, py = lax.div(piece, 4), lax.rem(piece, 4)
        return remote(
            self.away.at[px, py], self.near.at[px, py], self.cs.at[piece], self.cr.at[piece], 2 * z + 1 - c, d
        )

    def give(self, piece):
        c = self.spot[3]
        px, py = lax.div(piece, 4), lax.rem(piece, 4)

        def rows(row):
            self.away[px, py, row] = self.block(piece, row, 1 - c).astype(BF16)

        loop(0, NZ, rows)
        self.across(piece).start()

    def take(self, piece):
        c = self.spot[3]
        px, py = lax.div(piece, 4), lax.rem(piece, 4)
        self.across(piece).wait_recv()

        def rows(row):
            here = self.block(piece, row, c) + self.near[px, py, row].astype(F32)
            self.half[px, py, row] = here.astype(BF16)

        loop(0, NZ, rows)

    def clear(self):
        def rows(row):
            self.half[3, 3, row] = jnp.zeros((ROWS, 128), BF16)

        loop(0, NZ, rows)

    def cut(self, h, stage, where, low, count):
        q = self.spot[5]
        x, y = lax.div(q, 4), lax.rem(q, 4)
        rows = pl.ds(low, count)
        axis_x = (h == 0) == (stage == 0)
        if stage == 0:
            return self.half.at[where, :, rows] if axis_x else self.half.at[:, where, rows]
        return self.half.at[where, y, rows] if axis_x else self.half.at[x, where, rows]

    def plane(self, h, step, way):
        s, d, z, c, hi, q = self.spot
        x, y = lax.div(q, 4), lax.rem(q, 4)
        stage, second = step // 2, step % 2
        axis_x = (h == 0) == (stage == 0)
        near = neighbours(x if axis_x else y)
        if second:
            piece = self.cut(h, stage, near[way], 4 * h, 4)
        else:
            piece = self.cut(h, stage, near[2], 4 * h + 2 * way, 2)
        landing = ((self.a1, self.a2), (self.b1, self.b2))[stage][second].at[h, way]
        to = plane_device(h, stage, way, hi, x, y)
        return remote(piece, landing, self.ps.at[h, step, way], self.pr.at[h, step, way], s, to)

    def add(self, h, step):
        q = self.spot[5]
        x, y = lax.div(q, 4), lax.rem(q, 4)
        stage, second = step // 2, step % 2
        axis_x = (h == 0) == (stage == 0)
        me = x if axis_x else y
        near = neighbours(me)
        landing = ((self.a1, self.a2), (self.b1, self.b2))[stage][second]

        def spot_of(where, a, row):
            if stage == 0:
                return (where, a, row) if axis_x else (a, where, row)
            return (where, y, row) if axis_x else (x, where, row)

        def one(t):
            a, r = (lax.div(t, 4 if second else 2), lax.rem(t, 4 if second else 2))
            if second:
                at = spot_of(me, a, 4 * h + r)
                total = self.half[at].astype(F32)
                for way in range(2):
                    total += (landing[h, way, a, r] if stage == 0 else landing[h, way, r]).astype(F32)
                self.half[at] = total.astype(BF16)
            else:
                for way in range(2):
                    at = spot_of(near[way], a, 4 * h + 2 * way + r)
                    here = landing[h, way, a, r] if stage == 0 else landing[h, way, r]
                    self.half[at] = (self.half[at].astype(F32) + here.astype(F32)).astype(BF16)

        loop(0, (4 if stage == 0 else 1) * (4 if second else 2), one)

    def on_line(self, i):
        s, d, z, c, hi, q = self.spot
        t = lax.rem(hi * NZ + z + i, 2 * NZ)
        return 2 * lax.rem(t, NZ) + c, lax.div(t, NZ) * NXY + q, lax.rem(t, NZ)

    def along(self, i):
        q = self.spot[5]
        seq, dp, row = self.on_line(i)
        source = self.half.at[lax.div(q, 4), lax.rem(q, 4), row]
        return remote(source, self.column.at[i - 1], self.zs.at[i - 1], self.zr.at[i - 1], seq, dp)

    def spread(self, i):
        s, d, z, c, hi, q = self.spot
        to = hi * NXY + lax.rem(q + i, NXY)
        return remote(self.out.at[q], self.out.at[q], self.ss.at[i - 1], self.sr.at[i - 1], s, to)

    def sum_up(self):
        s, d, z, c, hi, q = self.spot
        loop(0, 15, self.take)
        for step in range(4):
            for h in range(2):
                if step:
                    for way in range(2):
                        self.plane(h, step - 1, way).wait_recv()
                    self.add(h, step - 1)
                for way in range(2):
                    self.plane(h, step, way).start()
        for h in range(2):
            for way in range(2):
                self.plane(h, 3, way).wait_recv()
            self.add(h, 3)
        loop(1, 2 * NZ, lambda i: self.along(i).start())
        loop(1, 2 * NZ, lambda i: self.along(i).wait_recv())
        total = self.half[lax.div(q, 4), lax.rem(q, 4), z].astype(F32)
        for i in range(1, 2 * NZ):
            total += self.column[i - 1].astype(F32)
        self.out[q] = total.astype(BF16)
        loop(1, NXY, lambda i: self.spread(i).start())
        loop(1, NXY, lambda i: self.spread(i).wait())

    def finish(self):
        loop(0, 15, lambda piece: self.across(piece).wait_send())
        for h in range(2):
            for step in range(4):
                for way in range(2):
                    self.plane(h, step, way).wait_send()
        loop(1, 2 * NZ, lambda i: self.along(i).wait_send())


def dot_last(a, b):
    return lax.dot_general(a, b, (((1,), (1,)), ((), ())), preferred_element_type=F32)


def dot_first(a, b):
    return lax.dot_general(a, b, (((0,), (0,)), ((), ())), preferred_element_type=F32)


def centred_of(tokens):
    values = tokens.astype(F32)
    centred = values - jnp.mean(values, axis=-1, keepdims=True)
    spread = jnp.mean(centred * centred, axis=-1, keepdims=True)
    return centred, lax.rsqrt(spread + epsilon)


def normalise(ch, f, tokens, cots, shift, scale, normed, cot):
    centred, rate = centred_of(tokens[ch, f])
    here = pl.ds(pl.multiple_of(ch * TOK + f * CP, CP), CP)
    normed[here, :] = (centred * rate * (1.0 + scale[...]) + shift[...]).astype(BF16)
    cot[pl.ds(pl.multiple_of(f * CP, CP), CP), :] = cots[ch, f]


def attention(ch, w, proj, gproj, normed, cot, acc, gnorm, block):
    rows = pl.ds(pl.multiple_of(ch * TOK, TOK), TOK)

    def project(i):
        proj[i] = jnp.dot(normed[rows, :], w[i], preferred_element_type=F32).astype(BF16)
        acc[i] = jnp.zeros((TOK, WIDE), F32)

    loop(0, 3, project)
    factor = HD ** (-0.5)

    def heads(a):
        lanes = pl.ds(pl.multiple_of(a * 128, 128), 256)
        query, key, value, grad = proj[0, :, lanes], proj[1, :, lanes], proj[2, :, lanes], cot[:, lanes]
        lane = lax.broadcasted_iota(jnp.int32, (TOK, 256), 1)
        for t in range(2):
            low = 16 * a + HD * t
            mask = jnp.where((lane >= low) & (lane < low + HD), 1.0, 0.0).astype(BF16)
            query_h, key_h, grad_h = query * mask, key * mask, grad * mask
            scores = dot_last(query_h, key) * factor + block[...]
            expo = jnp.exp(scores - jnp.max(scores, axis=-1, keepdims=True))
            attend = expo / jnp.sum(expo, axis=-1, keepdims=True)
            acc[2, :, lanes] += dot_first(attend.astype(BF16), grad_h)
            dots = dot_last(grad_h, value)
            gscores = attend * (dots - jnp.sum(attend * dots, axis=-1, keepdims=True)) * factor
            gscores = gscores.astype(BF16)
            acc[0, :, lanes] += jnp.dot(gscores, key_h, preferred_element_type=F32)
            acc[1, :, lanes] += dot_first(gscores, query_h)

    loop(0, 4, heads)

    def rounded(i):
        gproj[i, rows, :] = acc[i].astype(BF16)

    loop(0, 3, rounded)

    def grad_normed(n):
        part = pl.ds(pl.multiple_of(n * 384, 128), 384)
        total = dot_last(gproj[0, rows, :], w[0, part, :])
        total += dot_last(gproj[1, rows, :], w[1, part, :])
        total += dot_last(gproj[2, rows, :], w[2, part, :])
        gnorm[:, part] = total

    loop(0, 3, grad_normed)


def grad_tokens(ch, f, tokens, away, scale, gnorm):
    centred, rate = centred_of(tokens[ch, f])
    unit = centred * rate
    grad = gnorm[pl.ds(pl.multiple_of(f * CP, CP), CP), :] * (1.0 + scale[...])
    mean = jnp.mean(grad, axis=-1, keepdims=True)
    along = jnp.mean(grad * unit, axis=-1, keepdims=True)
    away[ch, f] = (rate * (grad - mean - unit * along)).astype(BF16)


def weight_partial(ch, i, normed, gproj, gw):
    rows = pl.ds(ch * TOK, TOK)

    def part(n):
        cut = pl.ds(pl.multiple_of(n * 384, 128), 384)
        term = dot_first(normed[rows, cut], gproj[i, rows, :])
        if ch == 0:
            gw[i, cut, :] = term
        else:
            gw[i, cut, :] += term

    loop(0, 3, part)


def kernel(
    x, cot_in, shift, scale, wp, out, gout,
    tokens, cots, away, proj, gproj, normed, cot, acc, gnorm, block, w, gw,
    g1, g2, g3, far, near, half, a1, a2, b1, b2, column,
    sx, rx, sc, rc, sb, rb, own_sems,
    gzs, gzr, gps, gpr, gcs, gcr, rcs, rcr, rps, rpr, rzs, rzr, rss, rsr,
):
    spot = place()
    s, d, z, c, hi, q = spot
    weight = Gather((wp, w, g1, g2, g3, gzs, gzr, gps, gpr, gcs, gcr, own_sems.at[4]), spot)
    total = Reduce(
        (gw, gout, far, near, half, a1, a2, b1, b2, column, rcs, rcr, rps, rpr, rzs, rzr, rss, rsr), spot
    )
    loop(1, SEQ, lambda i: greet(lax.rem(s + i, SEQ), d))
    loop(1, NXY, lambda i: greet(s, hi * NXY + lax.rem(q + i, NXY)))
    loop(0, NZ, lambda i: greet(2 * i + c, (1 - hi) * NXY + q))
    pl.semaphore_wait(pltpu.get_barrier_semaphore(), SEQ - 1 + NXY - 1 + NZ)

    def rows_of(j, ch):
        return pl.ds(pl.multiple_of(j * OWN + ch * CP, CP), CP)

    def send_x(ch, i):
        j = lax.rem(s + i, SEQ)
        return remote(x.at[rows_of(j, ch)], tokens.at[ch, s], sx.at[ch, i - 1], rx.at[ch, i - 1], j, d)

    def send_c(ch, i):
        j = lax.rem(s + i, SEQ)
        return remote(cot_in.at[rows_of(j, ch)], cots.at[ch, s], sc.at[ch, i - 1], rc.at[ch, i - 1], j, d)

    def send_back(ch, i):
        j = lax.rem(s + i, SEQ)
        return remote(away.at[ch, j], out.at[rows_of(s, ch)], sb.at[ch, i - 1], rb.at[ch, i - 1], j, d)

    def send_chunk(ch):
        def both(i):
            send_x(ch, i).start()
            send_c(ch, i).start()

        loop(1, SEQ, both)

    def between(step):
        if step == SECOND:
            send_chunk(1)

    weight.begin()
    send_chunk(0)
    keeps = []
    for ch in range(CH):
        keeps.append(pltpu.make_async_copy(x.at[rows_of(s, ch)], tokens.at[ch, s], own_sems.at[ch]))
        keeps.append(pltpu.make_async_copy(cot_in.at[rows_of(s, ch)], cots.at[ch, s], own_sems.at[CH + ch]))
    for keep in keeps:
        keep.start()
    weight.collect(between)
    row = lax.broadcasted_iota(jnp.int32, (TOK, TOK), 0)
    column_of = lax.broadcasted_iota(jnp.int32, (TOK, TOK), 1)
    block[...] = jnp.where(lax.rem(row, CP) == lax.rem(column_of, CP), 0.0, -1e30)
    for keep in keeps:
        keep.wait()
    total.clear()

    def chunk(ch):
        normalise(ch, s, tokens, cots, shift, scale, normed, cot)

        def arrived(i):
            send_x(ch, i).wait_recv()
            send_c(ch, i).wait_recv()
            normalise(ch, lax.rem(s + SEQ - i, SEQ), tokens, cots, shift, scale, normed, cot)

        loop(1, SEQ, arrived)
        attention(ch, w, proj, gproj, normed, cot, acc, gnorm, block)

        def leave(i):
            grad_tokens(ch, lax.rem(s + i, SEQ), tokens, away, scale, gnorm)
            send_back(ch, i).start()

        loop(1, SEQ, leave)
        grad_tokens(ch, s, tokens, away, scale, gnorm)
        mine = pltpu.make_async_copy(away.at[ch, s], out.at[rows_of(s, ch)], own_sems.at[0])
        mine.start()
        mine.wait()

    chunk(0)
    loop(0, 3, lambda i: weight_partial(0, i, normed, gproj, gw))
    chunk(1)

    def part(i):
        weight_partial(1, i, normed, gproj, gw)
        loop(0, 5, lambda t: total.give(5 * i + t))

    loop(0, 3, part)
    total.sum_up()
    total.finish()
    weight.finish()

    def finish(ch):
        def ends(i):
            send_x(ch, i).wait_send()
            send_c(ch, i).wait_send()
            send_back(ch, i).wait()

        loop(1, SEQ, ends)

    loop(0, CH, finish)


SECOND = 1


def fused(x, cot, shift, scale, wp):
    vm = pl.BlockSpec(memory_space=pltpu.VMEM)
    dma = pltpu.SemaphoreType.DMA
    return pl.pallas_call(
        kernel,
        out_shape=(jax.ShapeDtypeStruct((PATCH, D), BF16), jax.ShapeDtypeStruct((NQ, ROWS, 128), BF16)),
        in_specs=[vm] * 5,
        out_specs=(vm, vm),
        scratch_shapes=[
            pltpu.VMEM((CH, SEQ, CP, D), BF16),
            pltpu.VMEM((CH, SEQ, CP, WIDE), BF16),
            pltpu.VMEM((CH, SEQ, CP, D), BF16),
            pltpu.VMEM((3, TOK, WIDE), BF16),
            pltpu.VMEM((3, CH * TOK, WIDE), BF16),
            pltpu.VMEM((CH * TOK, D), BF16),
            pltpu.VMEM((TOK, WIDE), BF16),
            pltpu.VMEM((3, TOK, WIDE), F32),
            pltpu.VMEM((TOK, D), F32),
            pltpu.VMEM((TOK, TOK), F32),
            pltpu.VMEM((3, D, WIDE), BF16),
            pltpu.VMEM((3, D, WIDE), F32),
            pltpu.VMEM((NZ, ROWS, 128), BF16),
            pltpu.VMEM((4, 4, NZ, ROWS, 128), BF16),
            pltpu.VMEM((4, 4, NZ, ROWS, 128), BF16),
            pltpu.VMEM((4, 4, NZ, ROWS, 128), BF16),
            pltpu.VMEM((4, 4, NZ, ROWS, 128), BF16),
            pltpu.VMEM((4, 4, NZ, ROWS, 128), BF16),
            pltpu.VMEM((2, 2, 4, 2, ROWS, 128), BF16),
            pltpu.VMEM((2, 2, 4, 4, ROWS, 128), BF16),
            pltpu.VMEM((2, 2, 2, ROWS, 128), BF16),
            pltpu.VMEM((2, 2, 4, ROWS, 128), BF16),
            pltpu.VMEM((2 * NZ - 1, ROWS, 128), BF16),
        ]
        + [dma((CH, SEQ - 1))] * 6
        + [
            dma((5,)),
            dma((NZ - 1,)),
            dma((NZ - 1,)),
            dma((2, 4, 2)),
            dma((2, 4, 2)),
            dma((2, 7)),
            dma((2, 7)),
            dma((15,)),
            dma((15,)),
            dma((2, 4, 2)),
            dma((2, 4, 2)),
            dma((2 * NZ - 1,)),
            dma((2 * NZ - 1,)),
            dma((NXY - 1,)),
            dma((NXY - 1,)),
        ],
        compiler_params=pltpu.CompilerParams(
            collective_id=0, has_side_effects=True, vmem_limit_bytes=60 * 1024 * 1024
        ),
        name="temporal_backward",
    )(x, cot, shift, scale, wp)


def body(frames, shift_table, scale_table, grad_attended, w_qkv):
    wide = jnp.pad(w_qkv.reshape(ROWS, 3, INNER), ((0, 0), (0, 0), (0, WIDE - INNER)))
    wide = jnp.pad(wide.reshape(ROWS, 15, 128), ((0, 0), (0, 1), (0, 0)))
    cot = jnp.pad(grad_attended[0, 0], ((0, 0), (0, WIDE - INNER)))
    grad_tokens, total = fused(frames[0, 0], cot, shift_table, scale_table, wide.transpose(1, 0, 2))
    total = total[:15].transpose(1, 0, 2).reshape(ROWS, 3, WIDE)[:, :, :INNER]
    return grad_tokens[None, None], total.reshape(ROWS, 3 * INNER)


def solution(mesh):
    placed = (
        P("dp", "seq", None, None),
        P("dp", None),
        P("dp", None),
        P("dp", "seq", None, None),
        P("seq", None),
    )
    return jax.shard_map(
        body,
        mesh=mesh,
        in_specs=placed,
        out_specs=(P("dp", "seq", None, None), P("seq", None)),
        check_vma=False,
    )
```

```python
import jax
import jax.numpy as jnp
from jax import lax
from jax.experimental import pallas as pl
from jax.experimental.pallas import tpu as pltpu
from jax.sharding import PartitionSpec as P

MESH = pl.DeviceIdType.MESH
F32 = jnp.float32
BF16 = jnp.bfloat16

D = 1152
HD = 72
INNER = 576
WIDE = 640
SEQ = 16
NZ = 8
NXY = 16
NQ = 16
ROWS = 72
PATCH = 512
OWN = 32
CH = 4
CP = 8
GROUP = 4
TOK = SEQ * CP
epsilon = 1e-06


def place():
    s, d = lax.axis_index("seq"), lax.axis_index("dp")
    return s, d, lax.div(s, 2), lax.rem(s, 2), lax.div(d, NXY), lax.rem(d, NXY)


def remote(src, dst, send, recv, seq, dp):
    return pltpu.make_async_remote_copy(
        src_ref=src,
        dst_ref=dst,
        send_sem=send,
        recv_sem=recv,
        device_id={"seq": seq, "dp": dp},
        device_id_type=MESH,
    )


def loop(start, stop, body):
    def step(i, carry):
        body(i)
        return carry

    lax.fori_loop(start, stop, step, 0)


def greet(seq, dp):
    pl.semaphore_signal(
        pltpu.get_barrier_semaphore(),
        inc=1,
        device_id={"seq": seq, "dp": dp},
        device_id_type=MESH,
    )


def neighbours(me):
    return lax.rem(me + 1, 4), lax.rem(me + 3, 4), lax.rem(me + 2, 4)


def plane_device(h, stage, step, hi, x, y):
    along_x = (h == 0) == (stage == 0)
    me = x if along_x else y
    to = neighbours(me)[step]
    return hi * NXY + (to * 4 + y if along_x else x * 4 + to)


class Gather:
    def __init__(self, refs, spot):
        self.wp, self.w, self.g1, self.g2, self.g3, self.zs, self.zr, self.ps, self.pr, self.cs, self.cr, self.own = refs
        self.spot = spot

    def along_z(self, i):
        s, d, z, c, hi, q = self.spot
        four, at = lax.div(z, 4), lax.rem(z, 4)
        if isinstance(i, int) and i == 0:
            to = 2 * (4 * (1 - four) + at) + c
            return remote(self.wp.at[q], self.g1.at[four, at], self.zs.at[0], self.zr.at[0], to, d)
        to = 2 * (4 * four + lax.rem(at + i, 4)) + c
        return remote(self.g1.at[:, at], self.g1.at[:, at], self.zs.at[i], self.zr.at[i], to, d)

    def plane(self, h, step, way):
        s, d, z, c, hi, q = self.spot
        x, y = lax.div(q, 4), lax.rem(q, 4)
        stage, passes = step // 2, step % 2
        rows = pl.ds(2 * way, 2) if passes else slice(None)
        axis_x = (h == 0) == (stage == 0)
        other = neighbours(x if axis_x else y)[1 - way]
        if stage == 0:
            px, py = x, y
            if passes:
                px, py = (other, y) if axis_x else (x, other)
            piece = self.g2.at[px, py, h, rows]
        else:
            line = other if passes else (x if axis_x else y)
            piece = self.g2.at[line, :, h, rows] if axis_x else self.g2.at[:, line, h, rows]
        to = plane_device(h, stage, way, hi, x, y)
        return remote(piece, piece, self.ps.at[h, step, way], self.pr.at[h, step, way], s, to)

    def across(self, h, k):
        s, d, z, c, hi, q = self.spot
        x, y = lax.div(q, 4), lax.rem(q, 4)
        stage, which = k // 3, k % 3
        axis_x = (h == 0) == (stage == 0)
        other = neighbours(x if axis_x else y)[which]

        def region(ref):
            if stage == 0:
                return ref.at[other, y, h] if axis_x else ref.at[x, other, h]
            return ref.at[other, :, h] if axis_x else ref.at[:, other, h]

        return remote(
            region(self.g2), region(self.g3), self.cs.at[h, k], self.cr.at[h, k], 2 * z + 1 - c, d
        )

    def own_across(self):
        s, d, z, c, hi, q = self.spot
        x, y = lax.div(q, 4), lax.rem(q, 4)
        return remote(self.g2.at[x, y], self.g3.at[x, y], self.cs.at[0, 6], self.cr.at[0, 6], 2 * z + 1 - c, d)

    def begin(self):
        self.along_z(0).start()

    def collect(self, between):
        s, d, z, c, hi, q = self.spot
        x, y = lax.div(q, 4), lax.rem(q, 4)
        own = pltpu.make_async_copy(self.wp.at[q], self.g1.at[lax.div(z, 4), lax.rem(z, 4)], self.own)
        own.start()
        own.wait()
        self.along_z(0).wait_recv()
        loop(1, 4, lambda i: self.along_z(i).start())
        loop(1, 4, lambda i: self.along_z(i).wait_recv())
        own = pltpu.make_async_copy(self.g1, self.g2.at[x, y], self.own)
        own.start()
        own.wait()
        for step in range(4):
            for h in range(2):
                if step:
                    for way in range(2):
                        self.plane(h, step - 1, way).wait_recv()
                for way in range(2):
                    self.plane(h, step, way).start()
                if step == 0 and h == 0:
                    self.own_across().start()
                if step % 2:
                    for k in range(2):
                        self.across(h, 3 * (step // 2) + k).start()
                elif step:
                    self.across(h, 2).start()
            between(step)
        for h in range(2):
            for way in range(2):
                self.plane(h, 3, way).wait_recv()
            self.across(h, 5).start()
        self.own_across().wait_recv()
        for h in range(2):
            for k in range(6):
                self.across(h, k).wait_recv()

        def assemble(t):
            piece, row = lax.div(t, NZ), lax.rem(t, NZ)
            part, tile = lax.div(piece, 5), lax.rem(piece, 5)
            px, py = lax.div(piece, 4), lax.rem(piece, 4)
            here = self.g2[px, py, lax.div(row, 4), lax.rem(row, 4)].astype(F32)
            there = self.g3[px, py, lax.div(row, 4), lax.rem(row, 4)].astype(F32)
            both = jnp.concatenate([jnp.where(c == 0, here, there), jnp.where(c == 0, there, here)], axis=0)
            lanes = pl.ds(pl.multiple_of(tile * 128, 128), 128)
            self.w[part, pl.ds(pl.multiple_of(row * 144, 16), 144), lanes] = both.astype(BF16)

        loop(0, 15 * NZ, assemble)

    def finish(self):
        self.along_z(0).wait_send()
        loop(1, 4, lambda i: self.along_z(i).wait_send())
        self.own_across().wait_send()
        for h in range(2):
            for step in range(4):
                for way in range(2):
                    self.plane(h, step, way).wait_send()
            for k in range(6):
                self.across(h, k).wait_send()


class Reduce:
    def __init__(self, refs, spot):
        (self.gw, self.out, self.away, self.near, self.half, self.a1, self.a2, self.b1, self.b2, self.fours, self.column) = refs[:11]
        (self.cs, self.cr, self.ps, self.pr, self.zs, self.zr, self.ss, self.sr) = refs[11:]
        self.spot = spot

    def block(self, piece, row, core):
        part, tile = lax.div(piece, 5), lax.rem(piece, 5)
        first = pl.multiple_of(row * 144 + core * ROWS, 8)
        return self.gw[part, pl.ds(first, ROWS), pl.ds(pl.multiple_of(tile * 128, 128), 128)]

    def across(self, piece):
        s, d, z, c, hi, q = self.spot
        px, py = lax.div(piece, 4), lax.rem(piece, 4)
        return remote(
            self.away.at[px, py], self.near.at[px, py], self.cs.at[piece], self.cr.at[piece], 2 * z + 1 - c, d
        )

    def give(self, piece):
        c = self.spot[3]
        px, py = lax.div(piece, 4), lax.rem(piece, 4)

        def rows(row):
            self.away[px, py, row] = self.block(piece, row, 1 - c).astype(BF16)

        loop(0, NZ, rows)
        self.across(piece).start()

    def take(self, piece):
        c = self.spot[3]
        px, py = lax.div(piece, 4), lax.rem(piece, 4)
        self.across(piece).wait_recv()

        def rows(row):
            here = self.block(piece, row, c) + self.near[px, py, row].astype(F32)
            self.half[px, py, lax.div(row, 4), lax.rem(row, 4)] = here.astype(BF16)

        loop(0, NZ, rows)

    def clear(self):
        def rows(row):
            self.half[3, 3, lax.div(row, 4), lax.rem(row, 4)] = jnp.zeros((ROWS, 128), BF16)

        loop(0, NZ, rows)

    def cut(self, h, stage, where, low, count):
        q = self.spot[5]
        x, y = lax.div(q, 4), lax.rem(q, 4)
        rows = pl.ds(low, count)
        axis_x = (h == 0) == (stage == 0)
        if stage == 0:
            return self.half.at[where, :, h, rows] if axis_x else self.half.at[:, where, h, rows]
        return self.half.at[where, y, h, rows] if axis_x else self.half.at[x, where, h, rows]

    def plane(self, h, step, way):
        s, d, z, c, hi, q = self.spot
        x, y = lax.div(q, 4), lax.rem(q, 4)
        stage, second = step // 2, step % 2
        axis_x = (h == 0) == (stage == 0)
        near = neighbours(x if axis_x else y)
        if second:
            piece = self.cut(h, stage, near[way], 0, 4)
        else:
            piece = self.cut(h, stage, near[2], 2 * way, 2)
        landing = ((self.a1, self.a2), (self.b1, self.b2))[stage][second].at[h, way]
        to = plane_device(h, stage, way, hi, x, y)
        return remote(piece, landing, self.ps.at[h, step, way], self.pr.at[h, step, way], s, to)

    def add(self, h, step):
        q = self.spot[5]
        x, y = lax.div(q, 4), lax.rem(q, 4)
        stage, second = step // 2, step % 2
        axis_x = (h == 0) == (stage == 0)
        me = x if axis_x else y
        near = neighbours(me)
        landing = ((self.a1, self.a2), (self.b1, self.b2))[stage][second]

        def spot_of(where, a, row):
            if stage == 0:
                return (where, a, h, row) if axis_x else (a, where, h, row)
            return (where, y, h, row) if axis_x else (x, where, h, row)

        def one(t):
            a, r = (lax.div(t, 4 if second else 2), lax.rem(t, 4 if second else 2))
            if second:
                at = spot_of(me, a, r)
                total = self.half[at].astype(F32)
                for way in range(2):
                    total += (landing[h, way, a, r] if stage == 0 else landing[h, way, r]).astype(F32)
                self.half[at] = total.astype(BF16)
            else:
                for way in range(2):
                    at = spot_of(near[way], a, 2 * way + r)
                    here = landing[h, way, a, r] if stage == 0 else landing[h, way, r]
                    self.half[at] = (self.half[at].astype(F32) + here.astype(F32)).astype(BF16)

        loop(0, (4 if stage == 0 else 1) * (4 if second else 2), one)

    def in_four(self, i):
        s, d, z, c, hi, q = self.spot
        there = lax.rem(lax.rem(z, 4) + i, 4)
        source = self.half.at[lax.div(q, 4), lax.rem(q, 4), :, there]
        to = 2 * (4 * lax.div(z, 4) + there) + c
        return remote(source, self.fours.at[i - 1], self.zs.at[i - 1], self.zr.at[i - 1], to, d)

    def far_off(self, k):
        s, d, z, c, hi, q = self.spot
        four, at = lax.div(z, 4), lax.rem(z, 4)
        block = four if k == 2 else 1 - four
        source = self.half.at[lax.div(q, 4), lax.rem(q, 4), block, at]
        to = 2 * (4 * block + at) + c
        dp = d if k == 0 else (1 - hi) * NXY + q
        return remote(source, self.column.at[k], self.zs.at[3 + k], self.zr.at[3 + k], to, dp)

    def spread(self, i):
        s, d, z, c, hi, q = self.spot
        to = hi * NXY + lax.rem(q + i, NXY)
        return remote(self.out.at[q], self.out.at[q], self.ss.at[i - 1], self.sr.at[i - 1], s, to)

    def sum_up(self, beside):
        s, d, z, c, hi, q = self.spot
        loop(0, 15, self.take)
        for step in range(4):
            for h in range(2):
                if step:
                    for way in range(2):
                        self.plane(h, step - 1, way).wait_recv()
                    self.add(h, step - 1)
                for way in range(2):
                    self.plane(h, step, way).start()
        for h in range(2):
            for way in range(2):
                self.plane(h, 3, way).wait_recv()
            self.add(h, 3)
        px, py, four, at = lax.div(q, 4), lax.rem(q, 4), lax.div(z, 4), lax.rem(z, 4)
        loop(1, 4, lambda i: self.in_four(i).start())
        loop(1, 4, lambda i: self.in_four(i).wait_recv())
        for block in range(2):
            total = self.half[px, py, block, at].astype(F32)
            for i in range(3):
                total += self.fours[i, block].astype(F32)
            self.half[px, py, block, at] = total.astype(BF16)
        for k in range(3):
            self.far_off(k).start()
        beside()
        for k in range(3):
            self.far_off(k).wait_recv()
        total = self.half[px, py, four, at].astype(F32)
        for k in range(3):
            total += self.column[k].astype(F32)
        self.out[q] = total.astype(BF16)
        loop(1, NXY, lambda i: self.spread(i).start())
        loop(1, NXY, lambda i: self.spread(i).wait())

    def finish(self):
        loop(0, 15, lambda piece: self.across(piece).wait_send())
        for h in range(2):
            for step in range(4):
                for way in range(2):
                    self.plane(h, step, way).wait_send()
        loop(1, 4, lambda i: self.in_four(i).wait_send())
        for k in range(3):
            self.far_off(k).wait_send()


def dot_last(a, b):
    return lax.dot_general(a, b, (((1,), (1,)), ((), ())), preferred_element_type=F32)


def dot_first(a, b):
    return lax.dot_general(a, b, (((0,), (0,)), ((), ())), preferred_element_type=F32)


def centred_of(tokens):
    values = tokens.astype(F32)
    centred = values - jnp.mean(values, axis=-1, keepdims=True)
    spread = jnp.mean(centred * centred, axis=-1, keepdims=True)
    return centred, lax.rsqrt(spread + epsilon)


def chunk_rows(ch):
    return pl.ds(pl.multiple_of(ch * TOK, TOK), TOK)


def normalise(ch, tokens, cots, shift, scale, normed, cot):
    def group(g):
        centred, rate = centred_of(tokens[ch, pl.ds(g * GROUP, GROUP)].astype(F32).reshape(GROUP * CP, D))
        here = pl.ds(pl.multiple_of(ch * TOK + g * GROUP * CP, GROUP * CP), GROUP * CP)
        normed[here, :] = (centred * rate * (1.0 + scale[...]) + shift[...]).astype(BF16)
        here = pl.ds(pl.multiple_of(g * GROUP * CP, GROUP * CP), GROUP * CP)
        pair = cots[lax.div(ch, 2), pl.ds(g * GROUP, GROUP)].astype(F32).reshape(GROUP * CP, 2 * INNER)
        cot[here, :INNER] = jnp.where(lax.rem(ch, 2) == 0, pair[:, :INNER], pair[:, INNER:]).astype(BF16)

    loop(0, SEQ // GROUP, group)


def attention(ch, w, proj, gproj, normed, cot, block):
    rows = chunk_rows(ch)
    for i in range(3):
        proj[i] = jnp.dot(normed[rows, :], w[i], preferred_element_type=F32).astype(BF16)
    factor = HD ** (-0.5)
    lane = lax.broadcasted_iota(jnp.int32, (TOK, 256), 1)
    upper = [None] * 3
    for a in range(4):
        lanes = pl.ds(128 * a, 256)
        masks = []
        for t in range(2):
            low = 16 * a + HD * t
            masks.append(jnp.where((lane >= low) & (lane < low + HD), 1.0, 0.0).astype(BF16))

        def two(values):
            return jnp.concatenate([values * mask for mask in masks], axis=0)

        key, value = proj[1, :, lanes], proj[2, :, lanes]
        queries, keys, grads = two(proj[0, :, lanes]), two(key), two(cot[:, lanes])
        scores = dot_last(queries, key) * factor + block[...]
        expo = jnp.exp(scores - jnp.max(scores, axis=-1, keepdims=True))
        attend = expo / jnp.sum(expo, axis=-1, keepdims=True)
        dots = dot_last(grads, value)
        gscores = attend * (dots - jnp.sum(attend * dots, axis=-1, keepdims=True)) * factor
        gscores = gscores.astype(BF16)
        side = jnp.concatenate([gscores[:TOK], gscores[TOK:]], axis=1)
        found = (
            jnp.dot(side, keys, preferred_element_type=F32),
            dot_first(gscores, queries),
            dot_first(attend.astype(BF16), grads),
        )
        for i in range(3):
            lower = found[i][:, :128] if a == 0 else found[i][:, :128] + upper[i]
            gproj[i, rows, pl.ds(128 * a, 128)] = lower.astype(BF16)
            upper[i] = found[i][:, 128:]
    for i in range(3):
        gproj[i, rows, pl.ds(512, 128)] = upper[i].astype(BF16)


def grad_normed(ch, w, gproj, gnorm):
    rows = chunk_rows(ch)

    def part(n):
        cut = pl.ds(pl.multiple_of(n * 384, 128), 384)
        total = dot_last(gproj[0, rows, :], w[0, cut, :])
        total += dot_last(gproj[1, rows, :], w[1, cut, :])
        total += dot_last(gproj[2, rows, :], w[2, cut, :])
        gnorm[:, cut] = total

    loop(0, 3, part)


def grad_tokens(ch, g, tokens, away, scale, gnorm):
    frames = pl.ds(g * GROUP, GROUP)
    centred, rate = centred_of(tokens[ch, frames].astype(F32).reshape(GROUP * CP, D))
    unit = centred * rate
    grad = gnorm[pl.ds(pl.multiple_of(g * GROUP * CP, GROUP * CP), GROUP * CP), :] * (1.0 + scale[...])
    mean = jnp.mean(grad, axis=-1, keepdims=True)
    along = jnp.mean(grad * unit, axis=-1, keepdims=True)
    away[ch, frames] = (rate * (grad - mean - unit * along)).reshape(GROUP, CP, D).astype(BF16)


def weight_partial(first, count, i, normed, gproj, gw):
    rows = pl.ds(first * TOK, count * TOK)

    def part(n):
        cut = pl.ds(pl.multiple_of(n * 384, 128), 384)
        term = dot_first(normed[rows, cut], gproj[i, rows, :])
        if first == 0:
            gw[i, cut, :] = term
        else:
            gw[i, cut, :] += term

    loop(0, 3, part)


def narrow(parts):
    return jnp.concatenate([part[:, :INNER] for part in parts], axis=1)


def kernel(
    x, cot_in, shift, scale, w_in, out, gout,
    rows_in, turned, paired, wp, tiles, tokens, cots, away, proj, gproj, normed, cot, gnorm, block, w, gw,
    g1, g2, g3, far, near, half, a1, a2, b1, b2, fours, column,
    sx, rx, sc, rc, sb, rb, own_sems,
    gzs, gzr, gps, gpr, gcs, gcr, rcs, rcr, rps, rpr, rzs, rzr, rss, rsr,
):
    spot = place()
    s, d, z, c, hi, q = spot
    weight = Gather((wp, w, g1, g2, g3, gzs, gzr, gps, gpr, gcs, gcr, own_sems.at[0]), spot)
    total = Reduce(
        (gw, tiles, far, near, half, a1, a2, b1, b2, fours, column, rcs, rcr, rps, rpr, rzs, rzr, rss, rsr), spot
    )
    loop(1, SEQ, lambda i: greet(lax.rem(s + i, SEQ), d))
    loop(1, NXY, lambda i: greet(s, hi * NXY + lax.rem(q + i, NXY)))
    for at in (z, lax.rem(z + 4, NZ)):
        greet(2 * at + c, (1 - hi) * NXY + q)

    def group_of(j, ch):
        return j * CH + ch

    def send_x(ch, i):
        j = lax.rem(s + i, SEQ)
        return remote(x.at[group_of(j, ch)], tokens.at[ch, s], sx.at[ch, i - 1], rx.at[ch, i - 1], j, d)

    def send_c(pair, i):
        j = lax.rem(s + i, SEQ)
        return remote(paired.at[j, pair], cots.at[pair, s], sc.at[pair, i - 1], rc.at[pair, i - 1], j, d)

    def send_back(ch, i):
        j = lax.rem(s + i, SEQ)
        return remote(away.at[ch, j], out.at[group_of(s, ch)], sb.at[ch, i - 1], rb.at[ch, i - 1], j, d)

    def keep_back(ch):
        return pltpu.make_async_copy(away.at[ch, s], out.at[group_of(s, ch)], own_sems.at[1 + ch])

    def send_all(copy, k):
        loop(1, SEQ, lambda i: copy(k, i).start())

    def sent_all(copy, k):
        loop(1, SEQ, lambda i: copy(k, i).wait_send())

    def came_all(copy, k):
        loop(1, SEQ, lambda i: copy(k, i).wait_recv())

    def return_chunk(ch):
        loop(1, SEQ, lambda i: send_back(ch, i).start())
        keep_back(ch).start()

    load = pltpu.make_async_copy(w_in, rows_in, own_sems.at[0])
    turn = pltpu.make_async_copy(cot_in, turned, own_sems.at[1 + CH])
    load.start()
    turn.start()
    keeps = []
    for ch in range(CH):
        keeps.append(pltpu.make_async_copy(x.at[group_of(s, ch)], tokens.at[ch, s], own_sems.at[1 + ch]))
    for keep in keeps:
        keep.start()
    load.wait()
    pl.semaphore_wait(pltpu.get_barrier_semaphore(), SEQ - 1 + NXY - 1 + 2)

    gap = jnp.zeros((ROWS, WIDE - INNER), F32)
    for i in range(3):
        part = rows_in[:, pl.ds(i * INNER, INNER)].astype(F32)
        part = jnp.concatenate([part, gap], axis=1).astype(BF16)
        for t in range(5):
            wp[5 * i + t] = part[:, 128 * t : 128 * t + 128]
    wp[15] = jnp.zeros((ROWS, 128), BF16)
    weight.begin()
    send_all(send_x, 0)
    turn.wait()

    def pair_up(b):
        values = turned[:, pl.ds(pl.multiple_of(b * 128, 128), 128)].astype(F32).T
        values = values.reshape(4, 2, 2, CP, INNER)
        sides = jnp.concatenate([values[:, :, 0], values[:, :, 1]], axis=-1)
        paired[pl.ds(4 * b, 4)] = sides.astype(BF16)

    loop(0, 4, pair_up)
    send_all(send_c, 0)
    for pair in range(CH // 2):
        keeps.append(pltpu.make_async_copy(paired.at[s, pair], cots.at[pair, s], own_sems.at[1 + CH + pair]))
        keeps[-1].start()
    row = lax.broadcasted_iota(jnp.int32, (2 * TOK, TOK), 0)
    column_of = lax.broadcasted_iota(jnp.int32, (2 * TOK, TOK), 1)
    block[...] = jnp.where(lax.rem(row, CP) == lax.rem(column_of, CP), 0.0, -1e30)
    cot[:, pl.ds(512, 128)] = jnp.zeros((TOK, 128), BF16)
    total.clear()
    for keep in keeps:
        keep.wait()

    def between(step):
        if step == 0:
            send_all(send_x, 1)
        if step == 2:
            sent_all(send_x, 0)
            send_all(send_x, 2)
            send_all(send_c, 1)

    weight.collect(between)
    sent_all(send_x, 1)
    send_all(send_x, 3)

    def forward(ch):
        came_all(send_x, ch)

        @pl.when(lax.rem(ch, 2) == 0)
        def _():
            came_all(send_c, lax.div(ch, 2))

        normalise(ch, tokens, cots, shift, scale, normed, cot)
        attention(ch, w, proj, gproj, normed, cot, block)

    def backward(ch):
        grad_normed(ch, w, gproj, gnorm)
        loop(0, SEQ // GROUP, lambda g: grad_tokens(ch, g, tokens, away, scale, gnorm))

    def early(ch):
        forward(ch)
        backward(ch)

        @pl.when(ch == 1)
        def _():
            loop(0, 3, lambda i: weight_partial(0, 2, i, normed, gproj, gw))

    loop(0, 3, early)
    loop(0, 3, lambda i: weight_partial(2, 1, i, normed, gproj, gw))
    sent_all(send_x, 2)
    sent_all(send_x, 3)
    return_chunk(0)
    forward(3)

    def part(i):
        weight_partial(3, 1, i, normed, gproj, gw)
        loop(0, 5, lambda t: total.give(5 * i + t))

    loop(0, 3, part)
    return_chunk(1)
    backward(3)
    return_chunk(2)
    total.sum_up(lambda: return_chunk(3))
    gout[...] = narrow([jnp.concatenate([tiles[5 * i + t].astype(F32) for t in range(5)], axis=1) for i in range(3)]).astype(
        BF16
    )
    total.finish()
    weight.finish()
    for pair in range(CH // 2):
        sent_all(send_c, pair)

    def finish(ch):
        loop(1, SEQ, lambda i: send_back(ch, i).wait())
        keep_back(ch).wait()

    loop(0, CH, finish)


def fused(x, cot, shift, scale, w):
    vm, hbm = pl.BlockSpec(memory_space=pltpu.VMEM), pl.BlockSpec(memory_space=pl.ANY)
    dma = pltpu.SemaphoreType.DMA
    return pl.pallas_call(
        kernel,
        out_shape=(jax.ShapeDtypeStruct(x.shape, BF16), jax.ShapeDtypeStruct((ROWS, 3 * INNER), BF16)),
        in_specs=[hbm, hbm, vm, vm, hbm],
        out_specs=(vm, vm),
        scratch_shapes=[
            pltpu.VMEM((ROWS, 3 * INNER), BF16),
            pltpu.VMEM((INNER, PATCH), BF16),
            pltpu.VMEM((SEQ, CH // 2, CP, 2 * INNER), BF16),
            pltpu.VMEM((NQ, ROWS, 128), BF16),
            pltpu.VMEM((NQ, ROWS, 128), BF16),
            pltpu.VMEM((CH, SEQ, CP, D), BF16),
            pltpu.VMEM((CH // 2, SEQ, CP, 2 * INNER), BF16),
            pltpu.VMEM((CH, SEQ, CP, D), BF16),
            pltpu.VMEM((3, TOK, WIDE), BF16),
            pltpu.VMEM((3, CH * TOK, WIDE), BF16),
            pltpu.VMEM((CH * TOK, D), BF16),
            pltpu.VMEM((TOK, WIDE), BF16),
            pltpu.VMEM((TOK, D), F32),
            pltpu.VMEM((2 * TOK, TOK), F32),
            pltpu.VMEM((3, D, WIDE), BF16),
            pltpu.VMEM((3, D, WIDE), F32),
            pltpu.VMEM((2, 4, ROWS, 128), BF16),
            pltpu.VMEM((4, 4, 2, 4, ROWS, 128), BF16),
            pltpu.VMEM((4, 4, 2, 4, ROWS, 128), BF16),
            pltpu.VMEM((4, 4, NZ, ROWS, 128), BF16),
            pltpu.VMEM((4, 4, NZ, ROWS, 128), BF16),
            pltpu.VMEM((4, 4, 2, 4, ROWS, 128), BF16),
            pltpu.VMEM((2, 2, 4, 2, ROWS, 128), BF16),
            pltpu.VMEM((2, 2, 4, 4, ROWS, 128), BF16),
            pltpu.VMEM((2, 2, 2, ROWS, 128), BF16),
            pltpu.VMEM((2, 2, 4, ROWS, 128), BF16),
            pltpu.VMEM((3, 2, ROWS, 128), BF16),
            pltpu.VMEM((3, ROWS, 128), BF16),
        ]
        + [dma((CH, SEQ - 1))] * 2
        + [dma((CH // 2, SEQ - 1))] * 2
        + [dma((CH, SEQ - 1))] * 2
        + [
            dma((1 + 2 * CH,)),
            dma((4,)),
            dma((4,)),
            dma((2, 4, 2)),
            dma((2, 4, 2)),
            dma((2, 7)),
            dma((2, 7)),
            dma((15,)),
            dma((15,)),
            dma((2, 4, 2)),
            dma((2, 4, 2)),
            dma((6,)),
            dma((6,)),
            dma((NXY - 1,)),
            dma((NXY - 1,)),
        ],
        compiler_params=pltpu.CompilerParams(
            collective_id=0, has_side_effects=True, vmem_limit_bytes=60 * 1024 * 1024
        ),
        name="temporal_backward",
    )(x, cot, shift, scale, w)


def body(frames, shift_table, scale_table, grad_attended, w_qkv):
    x = frames.reshape(SEQ * CH, CP, D)
    cot = grad_attended[0, 0].T
    grad_tokens, grad_weight = fused(x, cot, shift_table, scale_table, w_qkv)
    return grad_tokens.reshape(frames.shape), grad_weight


def solution(mesh):
    placed = (
        P("dp", "seq", None, None),
        P("dp", None),
        P("dp", None),
        P("dp", "seq", None, None),
        P("seq", None),
    )
    return jax.shard_map(
        body,
        mesh=mesh,
        in_specs=placed,
        out_specs=(P("dp", "seq", None, None), P("seq", None)),
        check_vma=False,
    )
```

```python
import jax
import jax.numpy as jnp
from jax import lax
from jax.experimental import pallas as pl
from jax.experimental.pallas import tpu as pltpu
from jax.sharding import PartitionSpec as P

MESH = pl.DeviceIdType.MESH
F32 = jnp.float32
BF16 = jnp.bfloat16

D = 1152
HD = 72
INNER = 576
WIDE = 640
SEQ = 16
NZ = 8
NXY = 16
NQ = 16
ROWS = 72
PATCH = 512
OWN = 32
CH = 4
CP = 8
GROUP = 4
TOK = SEQ * CP
epsilon = 1e-06


def place():
    s, d = lax.axis_index("seq"), lax.axis_index("dp")
    return s, d, lax.div(s, 2), lax.rem(s, 2), lax.div(d, NXY), lax.rem(d, NXY)


def remote(src, dst, send, recv, seq, dp):
    return pltpu.make_async_remote_copy(
        src_ref=src,
        dst_ref=dst,
        send_sem=send,
        recv_sem=recv,
        device_id={"seq": seq, "dp": dp},
        device_id_type=MESH,
    )


def loop(start, stop, body):
    def step(i, carry):
        body(i)
        return carry

    lax.fori_loop(start, stop, step, 0)


def greet(seq, dp):
    pl.semaphore_signal(
        pltpu.get_barrier_semaphore(),
        inc=1,
        device_id={"seq": seq, "dp": dp},
        device_id_type=MESH,
    )


def neighbours(me):
    return lax.rem(me + 1, 4), lax.rem(me + 3, 4), lax.rem(me + 2, 4)


def plane_device(h, stage, step, hi, x, y):
    along_x = (h == 0) == (stage == 0)
    me = x if along_x else y
    to = neighbours(me)[step]
    return hi * NXY + (to * 4 + y if along_x else x * 4 + to)


class Gather:
    def __init__(self, refs, spot):
        self.wp, self.w, self.g1, self.g2, self.g3, self.zs, self.zr, self.ps, self.pr, self.cs, self.cr, self.own = refs
        self.spot = spot

    def along_z(self, i):
        s, d, z, c, hi, q = self.spot
        four, at = lax.div(z, 4), lax.rem(z, 4)
        if isinstance(i, int) and i == 0:
            to = 2 * (4 * (1 - four) + at) + c
            return remote(self.wp.at[q], self.g1.at[four, at], self.zs.at[0], self.zr.at[0], to, d)
        to = 2 * (4 * four + lax.rem(at + i, 4)) + c
        return remote(self.g1.at[:, at], self.g1.at[:, at], self.zs.at[i], self.zr.at[i], to, d)

    def plane(self, h, step, way):
        s, d, z, c, hi, q = self.spot
        x, y = lax.div(q, 4), lax.rem(q, 4)
        stage, passes = step // 2, step % 2
        rows = pl.ds(2 * way, 2) if passes else slice(None)
        axis_x = (h == 0) == (stage == 0)
        other = neighbours(x if axis_x else y)[1 - way]
        if stage == 0:
            px, py = x, y
            if passes:
                px, py = (other, y) if axis_x else (x, other)
            piece = self.g2.at[px, py, h, rows]
        else:
            line = other if passes else (x if axis_x else y)
            piece = self.g2.at[line, :, h, rows] if axis_x else self.g2.at[:, line, h, rows]
        to = plane_device(h, stage, way, hi, x, y)
        return remote(piece, piece, self.ps.at[h, step, way], self.pr.at[h, step, way], s, to)

    def across(self, h, k):
        s, d, z, c, hi, q = self.spot
        x, y = lax.div(q, 4), lax.rem(q, 4)
        stage, which = k // 3, k % 3
        axis_x = (h == 0) == (stage == 0)
        other = neighbours(x if axis_x else y)[which]

        def region(ref):
            if stage == 0:
                return ref.at[other, y, h] if axis_x else ref.at[x, other, h]
            return ref.at[other, :, h] if axis_x else ref.at[:, other, h]

        return remote(
            region(self.g2), region(self.g3), self.cs.at[h, k], self.cr.at[h, k], 2 * z + 1 - c, d
        )

    def own_across(self):
        s, d, z, c, hi, q = self.spot
        x, y = lax.div(q, 4), lax.rem(q, 4)
        return remote(self.g2.at[x, y], self.g3.at[x, y], self.cs.at[0, 6], self.cr.at[0, 6], 2 * z + 1 - c, d)

    def begin(self):
        self.along_z(0).start()

    def collect(self, between):
        s, d, z, c, hi, q = self.spot
        x, y = lax.div(q, 4), lax.rem(q, 4)
        own = pltpu.make_async_copy(self.wp.at[q], self.g1.at[lax.div(z, 4), lax.rem(z, 4)], self.own)
        own.start()
        own.wait()
        between(-2)
        self.along_z(0).wait_recv()
        loop(1, 4, lambda i: self.along_z(i).start())
        between(-1)
        loop(1, 4, lambda i: self.along_z(i).wait_recv())
        own = pltpu.make_async_copy(self.g1, self.g2.at[x, y], self.own)
        own.start()
        own.wait()
        for step in range(4):
            for h in range(2):
                if step:
                    for way in range(2):
                        self.plane(h, step - 1, way).wait_recv()
                for way in range(2):
                    self.plane(h, step, way).start()
                if step == 0 and h == 0:
                    self.own_across().start()
                if step % 2:
                    for k in range(2):
                        self.across(h, 3 * (step // 2) + k).start()
                elif step:
                    self.across(h, 2).start()
            between(step)
        for h in range(2):
            for way in range(2):
                self.plane(h, 3, way).wait_recv()
            self.across(h, 5).start()
        between(4)
        self.own_across().wait_recv()
        for h in range(2):
            for k in range(6):
                self.across(h, k).wait_recv()

        def assemble(t):
            piece, row = lax.div(t, NZ), lax.rem(t, NZ)
            part, tile = lax.div(piece, 5), lax.rem(piece, 5)
            px, py = lax.div(piece, 4), lax.rem(piece, 4)
            here = self.g2[px, py, lax.div(row, 4), lax.rem(row, 4)].astype(F32)
            there = self.g3[px, py, lax.div(row, 4), lax.rem(row, 4)].astype(F32)
            both = jnp.concatenate([jnp.where(c == 0, here, there), jnp.where(c == 0, there, here)], axis=0)
            lanes = pl.ds(pl.multiple_of(tile * 128, 128), 128)
            self.w[part, pl.ds(pl.multiple_of(row * 144, 16), 144), lanes] = both.astype(BF16)

        loop(0, 15 * NZ, assemble)

    def finish(self):
        self.along_z(0).wait_send()
        loop(1, 4, lambda i: self.along_z(i).wait_send())
        self.own_across().wait_send()
        for h in range(2):
            for step in range(4):
                for way in range(2):
                    self.plane(h, step, way).wait_send()
            for k in range(6):
                self.across(h, k).wait_send()


class Reduce:
    def __init__(self, refs, spot):
        (self.gw, self.out, self.away, self.near, self.half, self.a1, self.a2, self.b1, self.b2, self.fours, self.column) = refs[:11]
        (self.cs, self.cr, self.ps, self.pr, self.zs, self.zr, self.ss, self.sr) = refs[11:]
        self.spot = spot

    def block(self, piece, row, core):
        part, tile = lax.div(piece, 5), lax.rem(piece, 5)
        first = pl.multiple_of(row * 144 + core * ROWS, 8)
        return self.gw[part, pl.ds(first, ROWS), pl.ds(pl.multiple_of(tile * 128, 128), 128)]

    def across(self, piece):
        s, d, z, c, hi, q = self.spot
        px, py = lax.div(piece, 4), lax.rem(piece, 4)
        return remote(
            self.away.at[px, py], self.near.at[px, py], self.cs.at[piece], self.cr.at[piece], 2 * z + 1 - c, d
        )

    def give(self, piece):
        c = self.spot[3]
        px, py = lax.div(piece, 4), lax.rem(piece, 4)

        def rows(row):
            self.away[px, py, row] = self.block(piece, row, 1 - c).astype(BF16)

        loop(0, NZ, rows)
        self.across(piece).start()

    def take(self, piece):
        c = self.spot[3]
        px, py = lax.div(piece, 4), lax.rem(piece, 4)
        self.across(piece).wait_recv()

        def rows(row):
            here = self.block(piece, row, c) + self.near[px, py, row].astype(F32)
            self.half[px, py, lax.div(row, 4), lax.rem(row, 4)] = here.astype(BF16)

        loop(0, NZ, rows)

    def clear(self):
        def rows(row):
            self.half[3, 3, lax.div(row, 4), lax.rem(row, 4)] = jnp.zeros((ROWS, 128), BF16)

        loop(0, NZ, rows)

    def cut(self, h, stage, where, low, count):
        q = self.spot[5]
        x, y = lax.div(q, 4), lax.rem(q, 4)
        rows = pl.ds(low, count)
        axis_x = (h == 0) == (stage == 0)
        if stage == 0:
            return self.half.at[where, :, h, rows] if axis_x else self.half.at[:, where, h, rows]
        return self.half.at[where, y, h, rows] if axis_x else self.half.at[x, where, h, rows]

    def plane(self, h, step, way):
        s, d, z, c, hi, q = self.spot
        x, y = lax.div(q, 4), lax.rem(q, 4)
        stage, second = step // 2, step % 2
        axis_x = (h == 0) == (stage == 0)
        near = neighbours(x if axis_x else y)
        if second:
            piece = self.cut(h, stage, near[way], 0, 4)
        else:
            piece = self.cut(h, stage, near[2], 2 * way, 2)
        landing = ((self.a1, self.a2), (self.b1, self.b2))[stage][second].at[h, way]
        to = plane_device(h, stage, way, hi, x, y)
        return remote(piece, landing, self.ps.at[h, step, way], self.pr.at[h, step, way], s, to)

    def add(self, h, step):
        q = self.spot[5]
        x, y = lax.div(q, 4), lax.rem(q, 4)
        stage, second = step // 2, step % 2
        axis_x = (h == 0) == (stage == 0)
        me = x if axis_x else y
        near = neighbours(me)
        landing = ((self.a1, self.a2), (self.b1, self.b2))[stage][second]

        def spot_of(where, a, row):
            if stage == 0:
                return (where, a, h, row) if axis_x else (a, where, h, row)
            return (where, y, h, row) if axis_x else (x, where, h, row)

        def one(t):
            a, r = (lax.div(t, 4 if second else 2), lax.rem(t, 4 if second else 2))
            if second:
                at = spot_of(me, a, r)
                total = self.half[at].astype(F32)
                for way in range(2):
                    total += (landing[h, way, a, r] if stage == 0 else landing[h, way, r]).astype(F32)
                self.half[at] = total.astype(BF16)
            else:
                for way in range(2):
                    at = spot_of(near[way], a, 2 * way + r)
                    here = landing[h, way, a, r] if stage == 0 else landing[h, way, r]
                    self.half[at] = (self.half[at].astype(F32) + here.astype(F32)).astype(BF16)

        loop(0, (4 if stage == 0 else 1) * (4 if second else 2), one)

    def in_four(self, i):
        s, d, z, c, hi, q = self.spot
        there = lax.rem(lax.rem(z, 4) + i, 4)
        source = self.half.at[lax.div(q, 4), lax.rem(q, 4), :, there]
        to = 2 * (4 * lax.div(z, 4) + there) + c
        return remote(source, self.fours.at[i - 1], self.zs.at[i - 1], self.zr.at[i - 1], to, d)

    def far_off(self, k):
        s, d, z, c, hi, q = self.spot
        four, at = lax.div(z, 4), lax.rem(z, 4)
        block = four if k == 2 else 1 - four
        source = self.half.at[lax.div(q, 4), lax.rem(q, 4), block, at]
        to = 2 * (4 * block + at) + c
        dp = d if k == 0 else (1 - hi) * NXY + q
        return remote(source, self.column.at[k], self.zs.at[3 + k], self.zr.at[3 + k], to, dp)

    def spread(self, i):
        s, d, z, c, hi, q = self.spot
        to = hi * NXY + lax.rem(q + i, NXY)
        return remote(self.out.at[q], self.out.at[q], self.ss.at[i - 1], self.sr.at[i - 1], s, to)

    def sum_up(self, beside):
        s, d, z, c, hi, q = self.spot
        loop(0, 15, self.take)
        for step in range(4):
            for h in range(2):
                if step:
                    for way in range(2):
                        self.plane(h, step - 1, way).wait_recv()
                    self.add(h, step - 1)
                for way in range(2):
                    self.plane(h, step, way).start()
            beside(step)
        for h in range(2):
            for way in range(2):
                self.plane(h, 3, way).wait_recv()
            self.add(h, 3)
        px, py, four, at = lax.div(q, 4), lax.rem(q, 4), lax.div(z, 4), lax.rem(z, 4)
        loop(1, 4, lambda i: self.in_four(i).start())
        beside(4)
        loop(1, 4, lambda i: self.in_four(i).wait_recv())
        for block in range(2):
            total = self.half[px, py, block, at].astype(F32)
            for i in range(3):
                total += self.fours[i, block].astype(F32)
            self.half[px, py, block, at] = total.astype(BF16)
        for k in range(3):
            self.far_off(k).start()
        beside(5)
        for k in range(3):
            self.far_off(k).wait_recv()
        total = self.half[px, py, four, at].astype(F32)
        for k in range(3):
            total += self.column[k].astype(F32)
        self.out[q] = total.astype(BF16)
        loop(1, NXY, lambda i: self.spread(i).start())
        beside(6)
        loop(1, NXY, lambda i: self.spread(i).wait())

    def finish(self):
        loop(0, 15, lambda piece: self.across(piece).wait_send())
        for h in range(2):
            for step in range(4):
                for way in range(2):
                    self.plane(h, step, way).wait_send()
        loop(1, 4, lambda i: self.in_four(i).wait_send())
        for k in range(3):
            self.far_off(k).wait_send()


def dot_last(a, b):
    return lax.dot_general(a, b, (((1,), (1,)), ((), ())), preferred_element_type=F32)


def dot_first(a, b):
    return lax.dot_general(a, b, (((0,), (0,)), ((), ())), preferred_element_type=F32)


def centred_of(tokens):
    values = tokens.astype(F32)
    centred = values - jnp.mean(values, axis=-1, keepdims=True)
    spread = jnp.mean(centred * centred, axis=-1, keepdims=True)
    return centred, lax.rsqrt(spread + epsilon)


def chunk_rows(ch):
    return pl.ds(pl.multiple_of(ch * TOK, TOK), TOK)


def normalise(ch, tokens, cots, shift, scale, normed, cot):
    def group(g):
        centred, rate = centred_of(tokens[ch, pl.ds(g * GROUP, GROUP)].astype(F32).reshape(GROUP * CP, D))
        here = pl.ds(pl.multiple_of(ch * TOK + g * GROUP * CP, GROUP * CP), GROUP * CP)
        normed[here, :] = (centred * rate * (1.0 + scale[...]) + shift[...]).astype(BF16)
        here = pl.ds(pl.multiple_of(g * GROUP * CP, GROUP * CP), GROUP * CP)
        pair = cots[lax.div(ch, 2), pl.ds(g * GROUP, GROUP)].astype(F32).reshape(GROUP * CP, 2 * INNER)
        cot[here, :INNER] = jnp.where(lax.rem(ch, 2) == 0, pair[:, :INNER], pair[:, INNER:]).astype(BF16)

    loop(0, SEQ // GROUP, group)


def attention(ch, w, proj, gproj, normed, cot, block):
    rows = chunk_rows(ch)
    for i in range(3):
        proj[i] = jnp.dot(normed[rows, :], w[i], preferred_element_type=F32).astype(BF16)
    factor = HD ** (-0.5)
    lane = lax.broadcasted_iota(jnp.int32, (TOK, 256), 1)
    upper = [None] * 3
    for a in range(4):
        lanes = pl.ds(128 * a, 256)
        masks = []
        for t in range(2):
            low = 16 * a + HD * t
            masks.append(jnp.where((lane >= low) & (lane < low + HD), 1.0, 0.0).astype(BF16))

        def two(values):
            return jnp.concatenate([values * mask for mask in masks], axis=0)

        key, value = proj[1, :, lanes], proj[2, :, lanes]
        queries, keys, grads = two(proj[0, :, lanes]), two(key), two(cot[:, lanes])
        scores = dot_last(queries, key) * factor + block[...]
        expo = jnp.exp(scores - jnp.max(scores, axis=-1, keepdims=True))
        attend = expo / jnp.sum(expo, axis=-1, keepdims=True)
        dots = dot_last(grads, value)
        gscores = attend * (dots - jnp.sum(attend * dots, axis=-1, keepdims=True)) * factor
        gscores = gscores.astype(BF16)
        side = jnp.concatenate([gscores[:TOK], gscores[TOK:]], axis=1)
        found = (
            jnp.dot(side, keys, preferred_element_type=F32),
            dot_first(gscores, queries),
            dot_first(attend.astype(BF16), grads),
        )
        for i in range(3):
            lower = found[i][:, :128] if a == 0 else found[i][:, :128] + upper[i]
            gproj[i, rows, pl.ds(128 * a, 128)] = lower.astype(BF16)
            upper[i] = found[i][:, 128:]
    for i in range(3):
        gproj[i, rows, pl.ds(512, 128)] = upper[i].astype(BF16)


def grad_normed(ch, w, gproj, gnorm):
    rows = chunk_rows(ch)

    def part(n):
        cut = pl.ds(pl.multiple_of(n * 384, 128), 384)
        total = dot_last(gproj[0, rows, :], w[0, cut, :])
        total += dot_last(gproj[1, rows, :], w[1, cut, :])
        total += dot_last(gproj[2, rows, :], w[2, cut, :])
        gnorm[:, cut] = total

    loop(0, 3, part)


def grad_tokens(ch, g, tokens, away, scale, gnorm):
    frames = pl.ds(g * GROUP, GROUP)
    centred, rate = centred_of(tokens[ch, frames].astype(F32).reshape(GROUP * CP, D))
    unit = centred * rate
    grad = gnorm[pl.ds(pl.multiple_of(g * GROUP * CP, GROUP * CP), GROUP * CP), :] * (1.0 + scale[...])
    mean = jnp.mean(grad, axis=-1, keepdims=True)
    along = jnp.mean(grad * unit, axis=-1, keepdims=True)
    away[ch, frames] = (rate * (grad - mean - unit * along)).reshape(GROUP, CP, D).astype(BF16)


def weight_partial(first, count, i, normed, gproj, gw):
    rows = pl.ds(first * TOK, count * TOK)

    def part(n):
        cut = pl.ds(pl.multiple_of(n * 384, 128), 384)
        term = dot_first(normed[rows, cut], gproj[i, rows, :])
        if first == 0:
            gw[i, cut, :] = term
        else:
            gw[i, cut, :] += term

    loop(0, 3, part)


def narrow(parts):
    return jnp.concatenate([part[:, :INNER] for part in parts], axis=1)


def kernel(
    x, cot_in, shift, scale, w_in, out, gout,
    rows_in, turned, paired, wp, tiles, tokens, cots, away, proj, gproj, normed, cot, gnorm, block, w, gw,
    g1, g2, g3, far, near, half, a1, a2, b1, b2, fours, column,
    sx, rx, sc, rc, sb, rb, own_sems,
    gzs, gzr, gps, gpr, gcs, gcr, rcs, rcr, rps, rpr, rzs, rzr, rss, rsr,
):
    spot = place()
    s, d, z, c, hi, q = spot
    weight = Gather((wp, w, g1, g2, g3, gzs, gzr, gps, gpr, gcs, gcr, own_sems.at[0]), spot)
    total = Reduce(
        (gw, tiles, far, near, half, a1, a2, b1, b2, fours, column, rcs, rcr, rps, rpr, rzs, rzr, rss, rsr), spot
    )
    loop(1, SEQ, lambda i: greet(lax.rem(s + i, SEQ), d))
    loop(1, NXY, lambda i: greet(s, hi * NXY + lax.rem(q + i, NXY)))
    for at in (z, lax.rem(z + 4, NZ)):
        greet(2 * at + c, (1 - hi) * NXY + q)

    def group_of(j, ch):
        return j * CH + ch

    def send_x(ch, i):
        j = lax.rem(s + i, SEQ)
        return remote(x.at[group_of(j, ch)], tokens.at[ch, s], sx.at[ch, i - 1], rx.at[ch, i - 1], j, d)

    def send_c(pair, i):
        j = lax.rem(s + i, SEQ)
        return remote(paired.at[j, pair], cots.at[pair, s], sc.at[pair, i - 1], rc.at[pair, i - 1], j, d)

    def send_back(ch, i):
        j = lax.rem(s + i, SEQ)
        return remote(away.at[ch, j], out.at[group_of(s, ch)], sb.at[ch, i - 1], rb.at[ch, i - 1], j, d)

    def keep_back(ch):
        return pltpu.make_async_copy(away.at[ch, s], out.at[group_of(s, ch)], own_sems.at[1 + ch])

    def sent_all(copy, k):
        loop(1, SEQ, lambda i: copy(k, i).wait_send())

    def came_all(copy, k):
        loop(1, SEQ, lambda i: copy(k, i).wait_recv())

    order = ((send_x, 0), (send_c, 0), (send_x, 1), (send_x, 2), (send_c, 1), (send_x, 3))

    def feed(first, last):
        for k, (copy, which) in enumerate(order):
            low, high = max(first - 15 * k, 0), min(last - 15 * k, 15)
            if low < high:
                loop(low + 1, high + 1, lambda i: copy(which, i).start())

    def give_back(first, last):
        loop(first, last, lambda n: send_back(lax.div(n, 15), lax.rem(n, 15) + 1).start())

    load = pltpu.make_async_copy(w_in, rows_in, own_sems.at[0])
    turn = pltpu.make_async_copy(cot_in, turned, own_sems.at[1 + CH])
    load.start()
    turn.start()
    keeps = []
    for ch in range(CH):
        keeps.append(pltpu.make_async_copy(x.at[group_of(s, ch)], tokens.at[ch, s], own_sems.at[1 + ch]))
    for keep in keeps:
        keep.start()
    load.wait()
    pl.semaphore_wait(pltpu.get_barrier_semaphore(), SEQ - 1 + NXY - 1 + 2)

    gap = jnp.zeros((ROWS, WIDE - INNER), F32)
    for i in range(3):
        part = rows_in[:, pl.ds(i * INNER, INNER)].astype(F32)
        part = jnp.concatenate([part, gap], axis=1).astype(BF16)
        for t in range(5):
            wp[5 * i + t] = part[:, 128 * t : 128 * t + 128]
    wp[15] = jnp.zeros((ROWS, 128), BF16)
    weight.begin()

    def pair_up(b):
        values = turned[:, pl.ds(pl.multiple_of(b * 128, 128), 128)].astype(F32).T
        values = values.reshape(4, 2, 2, CP, INNER)
        sides = jnp.concatenate([values[:, :, 0], values[:, :, 1]], axis=-1)
        paired[pl.ds(4 * b, 4)] = sides.astype(BF16)

    def between(step):
        feed(FEEDS[step + 2], FEEDS[step + 3])
        if step == -2:
            turn.wait()
            loop(0, 2, pair_up)
        if step == -1:
            loop(2, 4, pair_up)
            for pair in range(CH // 2):
                keeps.append(
                    pltpu.make_async_copy(paired.at[s, pair], cots.at[pair, s], own_sems.at[1 + CH + pair])
                )
                keeps[-1].start()
        if step == 0:
            row = lax.broadcasted_iota(jnp.int32, (2 * TOK, TOK), 0)
            column_of = lax.broadcasted_iota(jnp.int32, (2 * TOK, TOK), 1)
            block[...] = jnp.where(lax.rem(row, CP) == lax.rem(column_of, CP), 0.0, -1e30)
            cot[:, pl.ds(512, 128)] = jnp.zeros((TOK, 128), BF16)
            total.clear()
            for keep in keeps:
                keep.wait()

    weight.collect(between)
    feed(FEEDS[7], 90)

    def forward(ch):
        came_all(send_x, ch)

        @pl.when(lax.rem(ch, 2) == 0)
        def _():
            came_all(send_c, lax.div(ch, 2))

        normalise(ch, tokens, cots, shift, scale, normed, cot)
        attention(ch, w, proj, gproj, normed, cot, block)

    def backward(ch):
        grad_normed(ch, w, gproj, gnorm)
        loop(0, SEQ // GROUP, lambda g: grad_tokens(ch, g, tokens, away, scale, gnorm))

    def early(ch):
        forward(ch)
        backward(ch)
        keep_back(ch).start()

        @pl.when(ch == 1)
        def _():
            loop(0, 3, lambda i: weight_partial(0, 2, i, normed, gproj, gw))

    loop(0, 3, early)
    loop(0, 3, lambda i: weight_partial(2, 1, i, normed, gproj, gw))
    sent_all(send_x, 3)
    give_back(0, RETURNS[0])
    forward(3)

    def part(i):
        weight_partial(3, 1, i, normed, gproj, gw)
        loop(0, 5, lambda t: total.give(5 * i + t))

    loop(0, 3, part)
    give_back(RETURNS[0], RETURNS[1])

    def beside(step):
        if step == 0:
            backward(3)
            keep_back(3).start()
        give_back(RETURNS[step + 1], RETURNS[step + 2])

    total.sum_up(beside)
    gout[...] = narrow([jnp.concatenate([tiles[5 * i + t].astype(F32) for t in range(5)], axis=1) for i in range(3)]).astype(
        BF16
    )
    total.finish()
    weight.finish()
    for pair in range(CH // 2):
        sent_all(send_c, pair)
    for ch in range(3):
        sent_all(send_x, ch)

    def finish(ch):
        loop(1, SEQ, lambda i: send_back(ch, i).wait())
        keep_back(ch).wait()

    loop(0, CH, finish)


FEEDS = (0, 6, 11, 16, 20, 30, 36, 40)
RETURNS = (10, 20, 25, 34, 39, 43, 47, 51, 60)


def fused(x, cot, shift, scale, w):
    vm, hbm = pl.BlockSpec(memory_space=pltpu.VMEM), pl.BlockSpec(memory_space=pl.ANY)
    dma = pltpu.SemaphoreType.DMA
    return pl.pallas_call(
        kernel,
        out_shape=(jax.ShapeDtypeStruct(x.shape, BF16), jax.ShapeDtypeStruct((ROWS, 3 * INNER), BF16)),
        in_specs=[hbm, hbm, vm, vm, hbm],
        out_specs=(vm, vm),
        scratch_shapes=[
            pltpu.VMEM((ROWS, 3 * INNER), BF16),
            pltpu.VMEM((INNER, PATCH), BF16),
            pltpu.VMEM((SEQ, CH // 2, CP, 2 * INNER), BF16),
            pltpu.VMEM((NQ, ROWS, 128), BF16),
            pltpu.VMEM((NQ, ROWS, 128), BF16),
            pltpu.VMEM((CH, SEQ, CP, D), BF16),
            pltpu.VMEM((CH // 2, SEQ, CP, 2 * INNER), BF16),
            pltpu.VMEM((CH, SEQ, CP, D), BF16),
            pltpu.VMEM((3, TOK, WIDE), BF16),
            pltpu.VMEM((3, CH * TOK, WIDE), BF16),
            pltpu.VMEM((CH * TOK, D), BF16),
            pltpu.VMEM((TOK, WIDE), BF16),
            pltpu.VMEM((TOK, D), F32),
            pltpu.VMEM((2 * TOK, TOK), F32),
            pltpu.VMEM((3, D, WIDE), BF16),
            pltpu.VMEM((3, D, WIDE), F32),
            pltpu.VMEM((2, 4, ROWS, 128), BF16),
            pltpu.VMEM((4, 4, 2, 4, ROWS, 128), BF16),
            pltpu.VMEM((4, 4, 2, 4, ROWS, 128), BF16),
            pltpu.VMEM((4, 4, NZ, ROWS, 128), BF16),
            pltpu.VMEM((4, 4, NZ, ROWS, 128), BF16),
            pltpu.VMEM((4, 4, 2, 4, ROWS, 128), BF16),
            pltpu.VMEM((2, 2, 4, 2, ROWS, 128), BF16),
            pltpu.VMEM((2, 2, 4, 4, ROWS, 128), BF16),
            pltpu.VMEM((2, 2, 2, ROWS, 128), BF16),
            pltpu.VMEM((2, 2, 4, ROWS, 128), BF16),
            pltpu.VMEM((3, 2, ROWS, 128), BF16),
            pltpu.VMEM((3, ROWS, 128), BF16),
        ]
        + [dma((CH, SEQ - 1))] * 2
        + [dma((CH // 2, SEQ - 1))] * 2
        + [dma((CH, SEQ - 1))] * 2
        + [
            dma((1 + 2 * CH,)),
            dma((4,)),
            dma((4,)),
            dma((2, 4, 2)),
            dma((2, 4, 2)),
            dma((2, 7)),
            dma((2, 7)),
            dma((15,)),
            dma((15,)),
            dma((2, 4, 2)),
            dma((2, 4, 2)),
            dma((6,)),
            dma((6,)),
            dma((NXY - 1,)),
            dma((NXY - 1,)),
        ],
        compiler_params=pltpu.CompilerParams(
            collective_id=0, has_side_effects=True, vmem_limit_bytes=60 * 1024 * 1024
        ),
        name="temporal_backward",
    )(x, cot, shift, scale, w)


def body(frames, shift_table, scale_table, grad_attended, w_qkv):
    x = frames.reshape(SEQ * CH, CP, D)
    cot = grad_attended[0, 0].T
    grad_tokens, grad_weight = fused(x, cot, shift_table, scale_table, w_qkv)
    return grad_tokens.reshape(frames.shape), grad_weight


def solution(mesh):
    placed = (
        P("dp", "seq", None, None),
        P("dp", None),
        P("dp", None),
        P("dp", "seq", None, None),
        P("seq", None),
    )
    return jax.shard_map(
        body,
        mesh=mesh,
        in_specs=placed,
        out_specs=(P("dp", "seq", None, None), P("seq", None)),
        check_vma=False,
    )
```

```python
import jax
import jax.numpy as jnp
from jax import lax
from jax.experimental import pallas as pl
from jax.experimental.pallas import tpu as pltpu
from jax.sharding import PartitionSpec as P

MESH = pl.DeviceIdType.MESH
F32 = jnp.float32
BF16 = jnp.bfloat16

D = 1152
HD = 72
INNER = 576
WIDE = 640
SEQ = 16
NZ = 8
NXY = 16
NQ = 16
ROWS = 72
PATCH = 512
OWN = 32
CH = 4
CP = 8
GROUP = 4
TOK = SEQ * CP
epsilon = 1e-06


def place():
    s, d = lax.axis_index("seq"), lax.axis_index("dp")
    return s, d, lax.div(s, 2), lax.rem(s, 2), lax.div(d, NXY), lax.rem(d, NXY)


def remote(src, dst, send, recv, seq, dp):
    return pltpu.make_async_remote_copy(
        src_ref=src,
        dst_ref=dst,
        send_sem=send,
        recv_sem=recv,
        device_id={"seq": seq, "dp": dp},
        device_id_type=MESH,
    )


def loop(start, stop, body):
    def step(i, carry):
        body(i)
        return carry

    lax.fori_loop(start, stop, step, 0)


def greet(seq, dp):
    pl.semaphore_signal(
        pltpu.get_barrier_semaphore(),
        inc=1,
        device_id={"seq": seq, "dp": dp},
        device_id_type=MESH,
    )


def neighbours(me):
    return lax.rem(me + 1, 4), lax.rem(me + 3, 4), lax.rem(me + 2, 4)


def plane_device(h, stage, step, hi, x, y):
    along_x = (h == 0) == (stage == 0)
    me = x if along_x else y
    to = neighbours(me)[step]
    return hi * NXY + (to * 4 + y if along_x else x * 4 + to)


class Gather:
    def __init__(self, refs, spot):
        self.wp, self.w, self.g1, self.g2, self.g3, self.zs, self.zr, self.ps, self.pr, self.cs, self.cr, self.own = refs
        self.spot = spot

    def along_z(self, i):
        s, d, z, c, hi, q = self.spot
        four, at = lax.div(z, 4), lax.rem(z, 4)
        if isinstance(i, int) and i == 0:
            to = 2 * (4 * (1 - four) + at) + c
            return remote(self.wp.at[q], self.g1.at[four, at], self.zs.at[0], self.zr.at[0], to, d)
        to = 2 * (4 * four + lax.rem(at + i, 4)) + c
        return remote(self.g1.at[:, at], self.g1.at[:, at], self.zs.at[i], self.zr.at[i], to, d)

    def plane(self, h, step, way):
        s, d, z, c, hi, q = self.spot
        x, y = lax.div(q, 4), lax.rem(q, 4)
        stage, passes = step // 2, step % 2
        rows = pl.ds(2 * way, 2) if passes else slice(None)
        axis_x = (h == 0) == (stage == 0)
        other = neighbours(x if axis_x else y)[1 - way]
        if stage == 0:
            px, py = x, y
            if passes:
                px, py = (other, y) if axis_x else (x, other)
            piece = self.g2.at[px, py, h, rows]
        else:
            line = other if passes else (x if axis_x else y)
            piece = self.g2.at[line, :, h, rows] if axis_x else self.g2.at[:, line, h, rows]
        to = plane_device(h, stage, way, hi, x, y)
        return remote(piece, piece, self.ps.at[h, step, way], self.pr.at[h, step, way], s, to)

    def across(self, h, k):
        s, d, z, c, hi, q = self.spot
        x, y = lax.div(q, 4), lax.rem(q, 4)
        stage, which = k // 3, k % 3
        axis_x = (h == 0) == (stage == 0)
        other = neighbours(x if axis_x else y)[which]

        def region(ref):
            if stage == 0:
                return ref.at[other, y, h] if axis_x else ref.at[x, other, h]
            return ref.at[other, :, h] if axis_x else ref.at[:, other, h]

        return remote(
            region(self.g2), region(self.g3), self.cs.at[h, k], self.cr.at[h, k], 2 * z + 1 - c, d
        )

    def own_across(self):
        s, d, z, c, hi, q = self.spot
        x, y = lax.div(q, 4), lax.rem(q, 4)
        return remote(self.g2.at[x, y], self.g3.at[x, y], self.cs.at[0, 6], self.cr.at[0, 6], 2 * z + 1 - c, d)

    def begin(self):
        self.along_z(0).start()

    def collect(self, between):
        s, d, z, c, hi, q = self.spot
        x, y = lax.div(q, 4), lax.rem(q, 4)
        own = pltpu.make_async_copy(self.wp.at[q], self.g1.at[lax.div(z, 4), lax.rem(z, 4)], self.own)
        own.start()
        own.wait()
        between(-2)
        self.along_z(0).wait_recv()
        loop(1, 4, lambda i: self.along_z(i).start())
        between(-1)
        loop(1, 4, lambda i: self.along_z(i).wait_recv())
        own = pltpu.make_async_copy(self.g1, self.g2.at[x, y], self.own)
        own.start()
        own.wait()
        for step in range(4):
            for h in range(2):
                if step:
                    for way in range(2):
                        self.plane(h, step - 1, way).wait_recv()
                for way in range(2):
                    self.plane(h, step, way).start()
                if step == 0 and h == 0:
                    self.own_across().start()
                if step % 2:
                    for k in range(2):
                        self.across(h, 3 * (step // 2) + k).start()
                elif step:
                    self.across(h, 2).start()
            between(step)
        for h in range(2):
            for way in range(2):
                self.plane(h, 3, way).wait_recv()
            self.across(h, 5).start()
        between(4)
        self.own_across().wait_recv()
        for h in range(2):
            for k in range(6):
                self.across(h, k).wait_recv()

        def assemble(t):
            piece, row = lax.div(t, NZ), lax.rem(t, NZ)
            part, tile = lax.div(piece, 5), lax.rem(piece, 5)
            px, py = lax.div(piece, 4), lax.rem(piece, 4)
            here = self.g2[px, py, lax.div(row, 4), lax.rem(row, 4)].astype(F32)
            there = self.g3[px, py, lax.div(row, 4), lax.rem(row, 4)].astype(F32)
            both = jnp.concatenate([jnp.where(c == 0, here, there), jnp.where(c == 0, there, here)], axis=0)
            lanes = pl.ds(pl.multiple_of(tile * 128, 128), 128)
            self.w[part, pl.ds(pl.multiple_of(row * 144, 16), 144), lanes] = both.astype(BF16)

        loop(0, 15 * NZ, assemble)

    def finish(self):
        self.along_z(0).wait_send()
        loop(1, 4, lambda i: self.along_z(i).wait_send())
        self.own_across().wait_send()
        for h in range(2):
            for step in range(4):
                for way in range(2):
                    self.plane(h, step, way).wait_send()
            for k in range(6):
                self.across(h, k).wait_send()


class Reduce:
    def __init__(self, refs, spot):
        (self.gw, self.out, self.away, self.near, self.half, self.a1, self.a2, self.b1, self.b2, self.fours, self.column) = refs[:11]
        (self.cs, self.cr, self.ps, self.pr, self.zs, self.zr, self.ss, self.sr) = refs[11:]
        self.spot = spot

    def block(self, piece, row, core):
        part, tile = lax.div(piece, 5), lax.rem(piece, 5)
        first = pl.multiple_of(row * 144 + core * ROWS, 8)
        return self.gw[part, pl.ds(first, ROWS), pl.ds(pl.multiple_of(tile * 128, 128), 128)]

    def lines(self, h, stage=0):
        q = self.spot[5]
        axis_x = (h == 0) == (stage == 0)
        me = lax.div(q, 4) if axis_x else lax.rem(q, 4)
        plus, minus, opposite = neighbours(me)
        return (opposite, plus, minus, me), axis_x

    def across(self, h, k):
        s, d, z, c, hi, q = self.spot
        places, axis_x = self.lines(h)

        def line(ref):
            return ref.at[places[k], :, h] if axis_x else ref.at[:, places[k], h]

        return remote(line(self.away), line(self.near), self.cs.at[h, k], self.cr.at[h, k], 2 * z + 1 - c, d)

    def each(self, h, k, body):
        places, axis_x = self.lines(h)

        def one(t):
            a, r = lax.div(t, 4), lax.rem(t, 4)
            px, py = (places[k], a) if axis_x else (a, places[k])
            body((px, py, h, r), jnp.minimum(4 * px + py, 14), 4 * h + r)

        loop(0, 16, one)

    def give(self, h, k):
        c = self.spot[3]

        def fill(at, piece, row):
            self.away[at] = self.block(piece, row, 1 - c).astype(BF16)

        self.each(h, k, fill)
        self.across(h, k).start()

    def take(self, h, k):
        c = self.spot[3]
        self.across(h, k).wait_recv()

        def fill(at, piece, row):
            self.half[at] = (self.block(piece, row, c) + self.near[at].astype(F32)).astype(BF16)

        self.each(h, k, fill)

    def plane(self, h, stage, part, way):
        s, d, z, c, hi, q = self.spot
        x, y = lax.div(q, 4), lax.rem(q, 4)
        places, axis_x = self.lines(h, stage)
        place = places[0] if part == 0 else places[1 + way]
        rows = pl.ds(2 * (1 - way) if part == 1 else 2 * way, 2)
        if stage == 0:
            piece = self.half.at[place, :, h, rows] if axis_x else self.half.at[:, place, h, rows]
            landing = self.a1.at[h, way] if part == 0 else self.a2.at[h, way, :, rows]
        else:
            piece = self.half.at[place, y, h, rows] if axis_x else self.half.at[x, place, h, rows]
            landing = self.b1.at[h, way] if part == 0 else self.b2.at[h, way, rows]
        at = (h, 3 * stage + part, way)
        return remote(piece, landing, self.ps.at[at], self.pr.at[at], s, plane_device(h, stage, way, hi, x, y))

    def add(self, h, stage, last):
        q = self.spot[5]
        x, y = lax.div(q, 4), lax.rem(q, 4)
        places, axis_x = self.lines(h, stage)

        def spot_of(place, a, row):
            if stage == 0:
                return (place, a, h, row) if axis_x else (a, place, h, row)
            return (place, y, h, row) if axis_x else (x, place, h, row)

        def one(t):
            if last:
                a, r = lax.div(t, 4), lax.rem(t, 4)
                at = spot_of(places[3], a, r)
                total = self.half[at].astype(F32)
                for way in range(2):
                    total += (self.a2[h, way, a, r] if stage == 0 else self.b2[h, way, r]).astype(F32)
                self.half[at] = total.astype(BF16)
            else:
                a, r = lax.div(t, 2), lax.rem(t, 2)
                for way in range(2):
                    at = spot_of(places[1 + way], a, 2 * way + r)
                    here = self.a1[h, way, a, r] if stage == 0 else self.b1[h, way, r]
                    self.half[at] = (self.half[at].astype(F32) + here.astype(F32)).astype(BF16)

        loop(0, (4 if stage == 0 else 1) * (4 if last else 2), one)

    def begin(self, beside):
        for k in range(4):
            for h in range(2):
                self.give(h, k)
                beside()

    def in_four(self, i):
        s, d, z, c, hi, q = self.spot
        there = lax.rem(lax.rem(z, 4) + i, 4)
        source = self.half.at[lax.div(q, 4), lax.rem(q, 4), :, there]
        to = 2 * (4 * lax.div(z, 4) + there) + c
        return remote(source, self.fours.at[i - 1], self.zs.at[i - 1], self.zr.at[i - 1], to, d)

    def far_off(self, k):
        s, d, z, c, hi, q = self.spot
        four, at = lax.div(z, 4), lax.rem(z, 4)
        block = four if k == 2 else 1 - four
        source = self.half.at[lax.div(q, 4), lax.rem(q, 4), block, at]
        to = 2 * (4 * block + at) + c
        dp = d if k == 0 else (1 - hi) * NXY + q
        return remote(source, self.column.at[k], self.zs.at[3 + k], self.zr.at[3 + k], to, dp)

    def spread(self, i):
        s, d, z, c, hi, q = self.spot
        to = hi * NXY + lax.rem(q + i, NXY)
        return remote(self.out.at[q], self.out.at[q], self.ss.at[i - 1], self.sr.at[i - 1], s, to)

    def sum_up(self, beside, between):
        s, d, z, c, hi, q = self.spot
        ways = [(h, way) for h in range(2) for way in range(2)]
        for stage in range(2):
            for part in range(2):
                for h in range(2):
                    if stage == 0:
                        for k in (0,) if part == 0 else (1, 2):
                            self.take(h, k)
                            beside()
                    for way in range(2):
                        self.plane(h, stage, part, way).start()
            if stage == 0:
                for h in range(2):
                    self.take(h, 3)
                    beside()
                between()
            beside()
            for h in range(2):
                for way in range(2):
                    self.plane(h, stage, 0, way).wait_recv()
                self.add(h, stage, False)
                for way in range(2):
                    self.plane(h, stage, 2, way).start()
            beside()
            for h in range(2):
                for way in range(2):
                    for part in (1, 2):
                        self.plane(h, stage, part, way).wait_recv()
                self.add(h, stage, True)
        px, py, four, at = lax.div(q, 4), lax.rem(q, 4), lax.div(z, 4), lax.rem(z, 4)
        loop(1, 4, lambda i: self.in_four(i).start())
        beside()
        loop(1, 4, lambda i: self.in_four(i).wait_recv())
        for block in range(2):
            total = self.half[px, py, block, at].astype(F32)
            for i in range(3):
                total += self.fours[i, block].astype(F32)
            self.half[px, py, block, at] = total.astype(BF16)
        for k in range(3):
            self.far_off(k).start()
        beside()
        for k in range(3):
            self.far_off(k).wait_recv()
        total = self.half[px, py, four, at].astype(F32)
        for k in range(3):
            total += self.column[k].astype(F32)
        self.out[q] = total.astype(BF16)
        loop(1, NXY, lambda i: self.spread(i).start())
        beside()
        loop(1, NXY, lambda i: self.spread(i).wait())

    def finish(self):
        for h in range(2):
            for k in range(4):
                self.across(h, k).wait_send()
            for stage in range(2):
                for part in range(3):
                    for way in range(2):
                        self.plane(h, stage, part, way).wait_send()
        loop(1, 4, lambda i: self.in_four(i).wait_send())
        for k in range(3):
            self.far_off(k).wait_send()


def dot_last(a, b):
    return lax.dot_general(a, b, (((1,), (1,)), ((), ())), preferred_element_type=F32)


def dot_first(a, b):
    return lax.dot_general(a, b, (((0,), (0,)), ((), ())), preferred_element_type=F32)


def centred_of(tokens):
    values = tokens.astype(F32)
    centred = values - jnp.mean(values, axis=-1, keepdims=True)
    spread = jnp.mean(centred * centred, axis=-1, keepdims=True)
    return centred, lax.rsqrt(spread + epsilon)


def chunk_rows(ch):
    return pl.ds(pl.multiple_of(ch * TOK, TOK), TOK)


def normalise(ch, tokens, cots, shift, scale, normed, cot):
    def group(g):
        centred, rate = centred_of(tokens[ch, pl.ds(g * GROUP, GROUP)].astype(F32).reshape(GROUP * CP, D))
        here = pl.ds(pl.multiple_of(ch * TOK + g * GROUP * CP, GROUP * CP), GROUP * CP)
        normed[here, :] = (centred * rate * (1.0 + scale[...]) + shift[...]).astype(BF16)
        here = pl.ds(pl.multiple_of(g * GROUP * CP, GROUP * CP), GROUP * CP)
        pair = cots[lax.div(ch, 2), pl.ds(g * GROUP, GROUP)].astype(F32).reshape(GROUP * CP, 2 * INNER)
        cot[here, :INNER] = jnp.where(lax.rem(ch, 2) == 0, pair[:, :INNER], pair[:, INNER:]).astype(BF16)

    loop(0, SEQ // GROUP, group)


def attention(ch, w, proj, gproj, normed, cot, block):
    rows = chunk_rows(ch)
    for i in range(3):
        proj[i] = jnp.dot(normed[rows, :], w[i], preferred_element_type=F32).astype(BF16)
    factor = HD ** (-0.5)
    lane = lax.broadcasted_iota(jnp.int32, (TOK, 256), 1)
    upper = [None] * 3
    for a in range(4):
        lanes = pl.ds(128 * a, 256)
        masks = []
        for t in range(2):
            low = 16 * a + HD * t
            masks.append(jnp.where((lane >= low) & (lane < low + HD), 1.0, 0.0).astype(BF16))

        def two(values):
            return jnp.concatenate([values * mask for mask in masks], axis=0)

        key, value = proj[1, :, lanes], proj[2, :, lanes]
        queries, keys, grads = two(proj[0, :, lanes]), two(key), two(cot[:, lanes])
        scores = dot_last(queries, key) * factor + block[...]
        expo = jnp.exp(scores - jnp.max(scores, axis=-1, keepdims=True))
        attend = expo / jnp.sum(expo, axis=-1, keepdims=True)
        dots = dot_last(grads, value)
        gscores = attend * (dots - jnp.sum(attend * dots, axis=-1, keepdims=True)) * factor
        gscores = gscores.astype(BF16)
        side = jnp.concatenate([gscores[:TOK], gscores[TOK:]], axis=1)
        found = (
            jnp.dot(side, keys, preferred_element_type=F32),
            dot_first(gscores, queries),
            dot_first(attend.astype(BF16), grads),
        )
        for i in range(3):
            lower = found[i][:, :128] if a == 0 else found[i][:, :128] + upper[i]
            gproj[i, rows, pl.ds(128 * a, 128)] = lower.astype(BF16)
            upper[i] = found[i][:, 128:]
    for i in range(3):
        gproj[i, rows, pl.ds(512, 128)] = upper[i].astype(BF16)


def grad_normed(ch, w, gproj, gnorm):
    rows = chunk_rows(ch)

    def part(n):
        cut = pl.ds(pl.multiple_of(n * 384, 128), 384)
        total = dot_last(gproj[0, rows, :], w[0, cut, :])
        total += dot_last(gproj[1, rows, :], w[1, cut, :])
        total += dot_last(gproj[2, rows, :], w[2, cut, :])
        gnorm[:, cut] = total

    loop(0, 3, part)


def grad_tokens(ch, g, tokens, away, scale, gnorm):
    frames = pl.ds(g * GROUP, GROUP)
    centred, rate = centred_of(tokens[ch, frames].astype(F32).reshape(GROUP * CP, D))
    unit = centred * rate
    grad = gnorm[pl.ds(pl.multiple_of(g * GROUP * CP, GROUP * CP), GROUP * CP), :] * (1.0 + scale[...])
    mean = jnp.mean(grad, axis=-1, keepdims=True)
    along = jnp.mean(grad * unit, axis=-1, keepdims=True)
    away[ch, frames] = (rate * (grad - mean - unit * along)).reshape(GROUP, CP, D).astype(BF16)


def weight_partial(first, count, normed, gproj, gw):
    rows = pl.ds(first * TOK, count * TOK)

    def part(n):
        cut = pl.ds(pl.multiple_of(n * 384, 128), 384)
        for i in range(3):
            term = dot_first(normed[rows, cut], gproj[i, rows, :])
            if first == 0:
                gw[i, cut, :] = term
            else:
                gw[i, cut, :] += term

    loop(0, 3, part)


def narrow(parts):
    return jnp.concatenate([part[:, :INNER] for part in parts], axis=1)


def kernel(
    x, cot_in, shift, scale, w_in, out, gout,
    rows_in, turned, paired, wp, tiles, tokens, cots, away, proj, gproj, normed, cot, gnorm, block, w, gw,
    g1, g2, g3, far, near, half, a1, a2, b1, b2, fours, column,
    sx, rx, sc, rc, sb, rb, own_sems,
    gzs, gzr, gps, gpr, gcs, gcr, rcs, rcr, rps, rpr, rzs, rzr, rss, rsr,
):
    spot = place()
    s, d, z, c, hi, q = spot
    weight = Gather((wp, w, g1, g2, g3, gzs, gzr, gps, gpr, gcs, gcr, own_sems.at[0]), spot)
    total = Reduce(
        (gw, tiles, far, near, half, a1, a2, b1, b2, fours, column, rcs, rcr, rps, rpr, rzs, rzr, rss, rsr), spot
    )
    loop(1, SEQ, lambda i: greet(lax.rem(s + i, SEQ), d))
    loop(1, NXY, lambda i: greet(s, hi * NXY + lax.rem(q + i, NXY)))
    for at in (z, lax.rem(z + 4, NZ)):
        greet(2 * at + c, (1 - hi) * NXY + q)

    def group_of(j, ch):
        return j * CH + ch

    def send_x(ch, i):
        j = lax.rem(s + i, SEQ)
        return remote(x.at[group_of(j, ch)], tokens.at[ch, s], sx.at[ch, i - 1], rx.at[ch, i - 1], j, d)

    def send_c(pair, i):
        j = lax.rem(s + i, SEQ)
        return remote(paired.at[j, pair], cots.at[pair, s], sc.at[pair, i - 1], rc.at[pair, i - 1], j, d)

    def send_back(ch, i):
        j = lax.rem(s + i, SEQ)
        return remote(away.at[ch, j], out.at[group_of(s, ch)], sb.at[ch, i - 1], rb.at[ch, i - 1], j, d)

    def keep_back(ch):
        return pltpu.make_async_copy(away.at[ch, s], out.at[group_of(s, ch)], own_sems.at[1 + ch])

    def sent_all(copy, k):
        loop(1, SEQ, lambda i: copy(k, i).wait_send())

    def came_all(copy, k):
        loop(1, SEQ, lambda i: copy(k, i).wait_recv())

    order = ((send_x, 0), (send_c, 0), (send_x, 1), (send_x, 2), (send_c, 1), (send_x, 3))

    def feed(first, last):
        for k, (copy, which) in enumerate(order):
            low, high = max(first - 15 * k, 0), min(last - 15 * k, 15)
            if low < high:
                loop(low + 1, high + 1, lambda i: copy(which, i).start())

    def give_back(first, last):
        loop(first, last, lambda n: send_back(lax.div(n, 15), lax.rem(n, 15) + 1).start())

    load = pltpu.make_async_copy(w_in, rows_in, own_sems.at[0])
    turn = pltpu.make_async_copy(cot_in, turned, own_sems.at[1 + CH])
    load.start()
    turn.start()
    keeps = []
    for ch in range(CH):
        keeps.append(pltpu.make_async_copy(x.at[group_of(s, ch)], tokens.at[ch, s], own_sems.at[1 + ch]))
    for keep in keeps:
        keep.start()
    load.wait()
    pl.semaphore_wait(pltpu.get_barrier_semaphore(), SEQ - 1 + NXY - 1 + 2)

    gap = jnp.zeros((ROWS, WIDE - INNER), F32)
    for i in range(3):
        part = rows_in[:, pl.ds(i * INNER, INNER)].astype(F32)
        part = jnp.concatenate([part, gap], axis=1).astype(BF16)
        for t in range(5):
            wp[5 * i + t] = part[:, 128 * t : 128 * t + 128]
    wp[15] = jnp.zeros((ROWS, 128), BF16)
    weight.begin()

    def pair_up(b):
        values = turned[:, pl.ds(pl.multiple_of(b * 128, 128), 128)].astype(F32).T
        values = values.reshape(4, 2, 2, CP, INNER)
        sides = jnp.concatenate([values[:, :, 0], values[:, :, 1]], axis=-1)
        paired[pl.ds(4 * b, 4)] = sides.astype(BF16)

    def between(step):
        feed(FEEDS[step + 2], FEEDS[step + 3])
        if step == -2:
            turn.wait()
            loop(0, 2, pair_up)
        if step == -1:
            loop(2, 4, pair_up)
            for pair in range(CH // 2):
                keeps.append(
                    pltpu.make_async_copy(paired.at[s, pair], cots.at[pair, s], own_sems.at[1 + CH + pair])
                )
                keeps[-1].start()
        if step == 0:
            row = lax.broadcasted_iota(jnp.int32, (2 * TOK, TOK), 0)
            column_of = lax.broadcasted_iota(jnp.int32, (2 * TOK, TOK), 1)
            block[...] = jnp.where(lax.rem(row, CP) == lax.rem(column_of, CP), 0.0, -1e30)
            cot[:, pl.ds(512, 128)] = jnp.zeros((TOK, 128), BF16)
            for keep in keeps:
                keep.wait()

    weight.collect(between)
    feed(FEEDS[7], 90)

    def forward(ch):
        came_all(send_x, ch)

        @pl.when(lax.rem(ch, 2) == 0)
        def _():
            came_all(send_c, lax.div(ch, 2))

        normalise(ch, tokens, cots, shift, scale, normed, cot)
        attention(ch, w, proj, gproj, normed, cot, block)

    def backward(ch):
        grad_normed(ch, w, gproj, gnorm)
        loop(0, SEQ // GROUP, lambda g: grad_tokens(ch, g, tokens, away, scale, gnorm))

    def early(ch):
        forward(ch)

        @pl.when(ch < 2)
        def _():
            backward(ch)
            keep_back(ch).start()

        @pl.when(ch == 1)
        def _():
            weight_partial(0, 2, normed, gproj, gw)

    loop(0, 3, early)
    weight_partial(2, 1, normed, gproj, gw)
    sent_all(send_x, 3)
    counts, started = iter(RETURNS), [0]

    def beside():
        first = started[0]
        started[0] = min(first + next(counts), 60)
        give_back(first, started[0])

    beside()
    forward(3)
    beside()
    weight_partial(3, 1, normed, gproj, gw)
    beside()
    total.begin(beside)

    def last_chunk():
        for ch in (2, 3):
            backward(ch)
            keep_back(ch).start()

    total.sum_up(beside, last_chunk)
    gout[...] = narrow([jnp.concatenate([tiles[5 * i + t].astype(F32) for t in range(5)], axis=1) for i in range(3)]).astype(
        BF16
    )
    total.finish()
    weight.finish()
    for pair in range(CH // 2):
        sent_all(send_c, pair)
    for ch in range(3):
        sent_all(send_x, ch)

    def finish(ch):
        loop(1, SEQ, lambda i: send_back(ch, i).wait())
        keep_back(ch).wait()

    loop(0, CH, finish)


FEEDS = (0, 8, 14, 20, 26, 38, 46, 52)
RETURNS = (10, 6, 6) + (0,) * 16 + (4, 5, 3, 3, 4, 4, 60)


def fused(x, cot, shift, scale, w):
    vm, hbm = pl.BlockSpec(memory_space=pltpu.VMEM), pl.BlockSpec(memory_space=pl.ANY)
    dma = pltpu.SemaphoreType.DMA
    return pl.pallas_call(
        kernel,
        out_shape=(jax.ShapeDtypeStruct(x.shape, BF16), jax.ShapeDtypeStruct((ROWS, 3 * INNER), BF16)),
        in_specs=[hbm, hbm, vm, vm, hbm],
        out_specs=(vm, vm),
        scratch_shapes=[
            pltpu.VMEM((ROWS, 3 * INNER), BF16),
            pltpu.VMEM((INNER, PATCH), BF16),
            pltpu.VMEM((SEQ, CH // 2, CP, 2 * INNER), BF16),
            pltpu.VMEM((NQ, ROWS, 128), BF16),
            pltpu.VMEM((NQ, ROWS, 128), BF16),
            pltpu.VMEM((CH, SEQ, CP, D), BF16),
            pltpu.VMEM((CH // 2, SEQ, CP, 2 * INNER), BF16),
            pltpu.VMEM((CH, SEQ, CP, D), BF16),
            pltpu.VMEM((3, TOK, WIDE), BF16),
            pltpu.VMEM((3, CH * TOK, WIDE), BF16),
            pltpu.VMEM((CH * TOK, D), BF16),
            pltpu.VMEM((TOK, WIDE), BF16),
            pltpu.VMEM((TOK, D), F32),
            pltpu.VMEM((2 * TOK, TOK), F32),
            pltpu.VMEM((3, D, WIDE), BF16),
            pltpu.VMEM((3, D, WIDE), F32),
            pltpu.VMEM((2, 4, ROWS, 128), BF16),
            pltpu.VMEM((4, 4, 2, 4, ROWS, 128), BF16),
            pltpu.VMEM((4, 4, 2, 4, ROWS, 128), BF16),
            pltpu.VMEM((4, 4, 2, 4, ROWS, 128), BF16),
            pltpu.VMEM((4, 4, 2, 4, ROWS, 128), BF16),
            pltpu.VMEM((4, 4, 2, 4, ROWS, 128), BF16),
            pltpu.VMEM((2, 2, 4, 2, ROWS, 128), BF16),
            pltpu.VMEM((2, 2, 4, 4, ROWS, 128), BF16),
            pltpu.VMEM((2, 2, 2, ROWS, 128), BF16),
            pltpu.VMEM((2, 2, 4, ROWS, 128), BF16),
            pltpu.VMEM((3, 2, ROWS, 128), BF16),
            pltpu.VMEM((3, ROWS, 128), BF16),
        ]
        + [dma((CH, SEQ - 1))] * 2
        + [dma((CH // 2, SEQ - 1))] * 2
        + [dma((CH, SEQ - 1))] * 2
        + [
            dma((1 + 2 * CH,)),
            dma((4,)),
            dma((4,)),
            dma((2, 4, 2)),
            dma((2, 4, 2)),
            dma((2, 7)),
            dma((2, 7)),
            dma((2, 4)),
            dma((2, 4)),
            dma((2, 6, 2)),
            dma((2, 6, 2)),
            dma((6,)),
            dma((6,)),
            dma((NXY - 1,)),
            dma((NXY - 1,)),
        ],
        compiler_params=pltpu.CompilerParams(
            collective_id=0, has_side_effects=True, vmem_limit_bytes=60 * 1024 * 1024
        ),
        name="temporal_backward",
    )(x, cot, shift, scale, w)


def body(frames, shift_table, scale_table, grad_attended, w_qkv):
    x = frames.reshape(SEQ * CH, CP, D)
    cot = grad_attended[0, 0].T
    grad_tokens, grad_weight = fused(x, cot, shift_table, scale_table, w_qkv)
    return grad_tokens.reshape(frames.shape), grad_weight


def solution(mesh):
    placed = (
        P("dp", "seq", None, None),
        P("dp", None),
        P("dp", None),
        P("dp", "seq", None, None),
        P("seq", None),
    )
    return jax.shard_map(
        body,
        mesh=mesh,
        in_specs=placed,
        out_specs=(P("dp", "seq", None, None), P("seq", None)),
        check_vma=False,
    )
```

```python
import jax
import jax.numpy as jnp
from jax import lax
from jax.experimental import pallas as pl
from jax.experimental.pallas import tpu as pltpu
from jax.sharding import PartitionSpec as P

MESH = pl.DeviceIdType.MESH
F32 = jnp.float32
BF16 = jnp.bfloat16

D = 1152
HD = 72
INNER = 576
WIDE = 640
SEQ = 16
NZ = 8
NXY = 16
NQ = 16
ROWS = 72
PATCH = 512
OWN = 32
CH = 4
CP = 8
GROUP = 4
TOK = SEQ * CP
epsilon = 1e-06


def place():
    s, d = lax.axis_index("seq"), lax.axis_index("dp")
    return s, d, lax.div(s, 2), lax.rem(s, 2), lax.div(d, NXY), lax.rem(d, NXY)


def remote(src, dst, send, recv, seq, dp):
    return pltpu.make_async_remote_copy(
        src_ref=src,
        dst_ref=dst,
        send_sem=send,
        recv_sem=recv,
        device_id={"seq": seq, "dp": dp},
        device_id_type=MESH,
    )


def loop(start, stop, body):
    def step(i, carry):
        body(i)
        return carry

    lax.fori_loop(start, stop, step, 0)


def wrap(place):
    return jnp.where(place >= 16, place - 16, place)


def greet(seq, dp):
    pl.semaphore_signal(
        pltpu.get_barrier_semaphore(),
        inc=1,
        device_id={"seq": seq, "dp": dp},
        device_id_type=MESH,
    )


def neighbours(me):
    return lax.rem(me + 1, 4), lax.rem(me + 3, 4), lax.rem(me + 2, 4)


def plane_device(h, stage, step, hi, x, y):
    along_x = (h == 0) == (stage == 0)
    me = x if along_x else y
    to = neighbours(me)[step]
    return hi * NXY + (to * 4 + y if along_x else x * 4 + to)


class Gather:
    def __init__(self, refs, spot):
        self.wp, self.w, self.g1, self.g2, self.g3, self.zs, self.zr, self.ps, self.pr, self.cs, self.cr, self.own = refs
        self.spot = spot

    def along_z(self, i):
        s, d, z, c, hi, q = self.spot
        four, at = lax.div(z, 4), lax.rem(z, 4)
        if isinstance(i, int) and i == 0:
            to = 2 * (4 * (1 - four) + at) + c
            return remote(self.wp.at[q], self.g1.at[four, at], self.zs.at[0], self.zr.at[0], to, d)
        to = 2 * (4 * four + lax.rem(at + i, 4)) + c
        return remote(self.g1.at[:, at], self.g1.at[:, at], self.zs.at[i], self.zr.at[i], to, d)

    def plane(self, h, step, way):
        s, d, z, c, hi, q = self.spot
        x, y = lax.div(q, 4), lax.rem(q, 4)
        stage, passes = step // 2, step % 2
        rows = pl.ds(2 * way, 2) if passes else slice(None)
        axis_x = (h == 0) == (stage == 0)
        other = neighbours(x if axis_x else y)[1 - way]
        if stage == 0:
            px, py = x, y
            if passes:
                px, py = (other, y) if axis_x else (x, other)
            piece = self.g2.at[px, py, h, rows]
        else:
            line = other if passes else (x if axis_x else y)
            piece = self.g2.at[line, :, h, rows] if axis_x else self.g2.at[:, line, h, rows]
        to = plane_device(h, stage, way, hi, x, y)
        return remote(piece, piece, self.ps.at[h, step, way], self.pr.at[h, step, way], s, to)

    def across(self, h, k):
        s, d, z, c, hi, q = self.spot
        x, y = lax.div(q, 4), lax.rem(q, 4)
        stage, which = k // 3, k % 3
        axis_x = (h == 0) == (stage == 0)
        other = neighbours(x if axis_x else y)[which]

        def region(ref):
            if stage == 0:
                return ref.at[other, y, h] if axis_x else ref.at[x, other, h]
            return ref.at[other, :, h] if axis_x else ref.at[:, other, h]

        return remote(
            region(self.g2), region(self.g3), self.cs.at[h, k], self.cr.at[h, k], 2 * z + 1 - c, d
        )

    def own_across(self):
        s, d, z, c, hi, q = self.spot
        x, y = lax.div(q, 4), lax.rem(q, 4)
        return remote(self.g2.at[x, y], self.g3.at[x, y], self.cs.at[0, 6], self.cr.at[0, 6], 2 * z + 1 - c, d)

    def begin(self):
        self.along_z(0).start()

    def collect(self, between):
        s, d, z, c, hi, q = self.spot
        x, y = lax.div(q, 4), lax.rem(q, 4)
        own = pltpu.make_async_copy(self.wp.at[q], self.g1.at[lax.div(z, 4), lax.rem(z, 4)], self.own)
        own.start()
        own.wait()
        between(-2)
        self.along_z(0).wait_recv()
        loop(1, 4, lambda i: self.along_z(i).start())
        between(-1)
        loop(1, 4, lambda i: self.along_z(i).wait_recv())
        own = pltpu.make_async_copy(self.g1, self.g2.at[x, y], self.own)
        own.start()
        own.wait()
        for step in range(4):
            for h in range(2):
                if step:
                    for way in range(2):
                        self.plane(h, step - 1, way).wait_recv()
                for way in range(2):
                    self.plane(h, step, way).start()
                if step == 0 and h == 0:
                    self.own_across().start()
                if step % 2:
                    for k in range(2):
                        self.across(h, 3 * (step // 2) + k).start()
                elif step:
                    self.across(h, 2).start()
            between(step)
        for h in range(2):
            for way in range(2):
                self.plane(h, 3, way).wait_recv()
            self.across(h, 5).start()
        between(4)
        self.own_across().wait_recv()
        for h in range(2):
            for k in range(6):
                self.across(h, k).wait_recv()

        def assemble(t):
            piece, row = lax.div(t, NZ), lax.rem(t, NZ)
            part, tile = lax.div(piece, 5), lax.rem(piece, 5)
            px, py = lax.div(piece, 4), lax.rem(piece, 4)
            here = self.g2[px, py, lax.div(row, 4), lax.rem(row, 4)].astype(F32)
            there = self.g3[px, py, lax.div(row, 4), lax.rem(row, 4)].astype(F32)
            both = jnp.concatenate([jnp.where(c == 0, here, there), jnp.where(c == 0, there, here)], axis=0)
            lanes = pl.ds(pl.multiple_of(tile * 128, 128), 128)
            self.w[part, pl.ds(pl.multiple_of(row * 144, 16), 144), lanes] = both.astype(BF16)

        loop(0, 15 * NZ, assemble)

    def finish(self):
        for i in range(4):
            self.along_z(i).wait_send()
        self.own_across().wait_send()
        for h in range(2):
            for step in range(4):
                for way in range(2):
                    self.plane(h, step, way).wait_send()
            for k in range(6):
                self.across(h, k).wait_send()


class Reduce:
    def __init__(self, refs, spot):
        (self.gw, self.out, self.away, self.near, self.half, self.a1, self.a2, self.b1, self.b2, self.fours, self.column) = refs[:11]
        (self.cs, self.cr, self.ps, self.pr, self.zs, self.zr, self.ss, self.sr) = refs[11:]
        self.spot = spot

    def block(self, piece, row, core):
        part, tile = lax.div(piece, 5), lax.rem(piece, 5)
        first = pl.multiple_of(row * 144 + core * ROWS, 8)
        return self.gw[part, pl.ds(first, ROWS), pl.ds(pl.multiple_of(tile * 128, 128), 128)]

    def lines(self, h, stage=0):
        q = self.spot[5]
        axis_x = (h == 0) == (stage == 0)
        me = lax.div(q, 4) if axis_x else lax.rem(q, 4)
        plus, minus, opposite = neighbours(me)
        return (opposite, plus, minus, me), axis_x

    def across(self, h, k):
        s, d, z, c, hi, q = self.spot
        places, axis_x = self.lines(h)

        def line(ref):
            return ref.at[places[k], :, h] if axis_x else ref.at[:, places[k], h]

        return remote(line(self.away), line(self.near), self.cs.at[h, k], self.cr.at[h, k], 2 * z + 1 - c, d)

    def each(self, h, k, body):
        places, axis_x = self.lines(h)

        def one(t):
            a, r = lax.div(t, 4), lax.rem(t, 4)
            px, py = (places[k], a) if axis_x else (a, places[k])
            body((px, py, h, r), jnp.minimum(4 * px + py, 14), 4 * h + r)

        loop(0, 16, one)

    def give(self, h, k):
        c = self.spot[3]

        def fill(at, piece, row):
            self.away[at] = self.block(piece, row, 1 - c).astype(BF16)

        self.each(h, k, fill)
        self.across(h, k).start()

    def take(self, h, k):
        c = self.spot[3]
        self.across(h, k).wait_recv()

        def fill(at, piece, row):
            self.half[at] = (self.block(piece, row, c) + self.near[at].astype(F32)).astype(BF16)

        self.each(h, k, fill)

    def plane(self, h, stage, part, way):
        s, d, z, c, hi, q = self.spot
        x, y = lax.div(q, 4), lax.rem(q, 4)
        places, axis_x = self.lines(h, stage)
        place = places[0] if part == 0 else places[1 + way]
        rows = pl.ds(2 * (1 - way) if part == 1 else 2 * way, 2)
        if stage == 0:
            piece = self.half.at[place, :, h, rows] if axis_x else self.half.at[:, place, h, rows]
            landing = self.a1.at[h, way] if part == 0 else self.a2.at[h, way, :, rows]
        else:
            piece = self.half.at[place, y, h, rows] if axis_x else self.half.at[x, place, h, rows]
            landing = self.b1.at[h, way] if part == 0 else self.b2.at[h, way, rows]
        at = (h, 3 * stage + part, way)
        return remote(piece, landing, self.ps.at[at], self.pr.at[at], s, plane_device(h, stage, way, hi, x, y))

    def add(self, h, stage, last):
        q = self.spot[5]
        x, y = lax.div(q, 4), lax.rem(q, 4)
        places, axis_x = self.lines(h, stage)

        def spot_of(place, a, row):
            if stage == 0:
                return (place, a, h, row) if axis_x else (a, place, h, row)
            return (place, y, h, row) if axis_x else (x, place, h, row)

        def one(t):
            if last:
                a, r = lax.div(t, 4), lax.rem(t, 4)
                at = spot_of(places[3], a, r)
                total = self.half[at].astype(F32)
                for way in range(2):
                    total += (self.a2[h, way, a, r] if stage == 0 else self.b2[h, way, r]).astype(F32)
                self.half[at] = total.astype(BF16)
            else:
                a, r = lax.div(t, 2), lax.rem(t, 2)
                for way in range(2):
                    at = spot_of(places[1 + way], a, 2 * way + r)
                    here = self.a1[h, way, a, r] if stage == 0 else self.b1[h, way, r]
                    self.half[at] = (self.half[at].astype(F32) + here.astype(F32)).astype(BF16)

        loop(0, (4 if stage == 0 else 1) * (4 if last else 2), one)

    def begin(self, beside):
        for k in range(4):
            for h in range(2):
                self.give(h, k)
                beside()

    def in_four(self, i):
        s, d, z, c, hi, q = self.spot
        there = lax.rem(lax.rem(z, 4) + i, 4)
        source = self.half.at[lax.div(q, 4), lax.rem(q, 4), :, there]
        to = 2 * (4 * lax.div(z, 4) + there) + c
        return remote(source, self.fours.at[i - 1], self.zs.at[i - 1], self.zr.at[i - 1], to, d)

    def far_off(self, k):
        s, d, z, c, hi, q = self.spot
        four, at = lax.div(z, 4), lax.rem(z, 4)
        block = four if k == 2 else 1 - four
        source = self.half.at[lax.div(q, 4), lax.rem(q, 4), block, at]
        to = 2 * (4 * block + at) + c
        dp = d if k == 0 else (1 - hi) * NXY + q
        return remote(source, self.column.at[k], self.zs.at[3 + k], self.zr.at[3 + k], to, dp)

    def spread(self, i):
        s, d, z, c, hi, q = self.spot
        to = hi * NXY + wrap(q + i)
        return remote(self.out.at[q], self.out.at[q], self.ss.at[i - 1], self.sr.at[i - 1], s, to)

    def sum_up(self, beside, between, settle):
        s, d, z, c, hi, q = self.spot
        ways = [(h, way) for h in range(2) for way in range(2)]
        for stage in range(2):
            for part in range(2):
                for h in range(2):
                    if stage == 0:
                        for k in (0,) if part == 0 else (1, 2):
                            self.take(h, k)
                            beside()
                    for way in range(2):
                        self.plane(h, stage, part, way).start()
            if stage == 0:
                for h in range(2):
                    self.take(h, 3)
                    beside()
                between()
            beside()
            for h in range(2):
                for way in range(2):
                    self.plane(h, stage, 0, way).wait_recv()
                self.add(h, stage, False)
                for way in range(2):
                    self.plane(h, stage, 2, way).start()
            beside()
            for h in range(2):
                for way in range(2):
                    for part in (1, 2):
                        self.plane(h, stage, part, way).wait_recv()
                self.add(h, stage, True)
        px, py, four, at = lax.div(q, 4), lax.rem(q, 4), lax.div(z, 4), lax.rem(z, 4)
        loop(1, 4, lambda i: self.in_four(i).start())
        beside()
        loop(1, 4, lambda i: self.in_four(i).wait_recv())
        for block in range(2):
            total = self.half[px, py, block, at].astype(F32)
            for i in range(3):
                total += self.fours[i, block].astype(F32)
            self.half[px, py, block, at] = total.astype(BF16)
        for k in range(3):
            self.far_off(k).start()
        beside()
        for k in range(3):
            self.far_off(k).wait_recv()
        total = self.half[px, py, four, at].astype(F32)
        for k in range(3):
            total += self.column[k].astype(F32)
        self.out[q] = total.astype(BF16)
        for i in range(1, NXY):
            self.spread(i).start()
        beside()
        settle()
        for i in range(1, NXY):
            self.spread(i).wait()

    def finish(self):
        for h in range(2):
            for k in range(4):
                self.across(h, k).wait_send()
            for stage in range(2):
                for part in range(3):
                    for way in range(2):
                        self.plane(h, stage, part, way).wait_send()
        loop(1, 4, lambda i: self.in_four(i).wait_send())
        for k in range(3):
            self.far_off(k).wait_send()


def dot_last(a, b):
    return lax.dot_general(a, b, (((1,), (1,)), ((), ())), preferred_element_type=F32)


def dot_first(a, b):
    return lax.dot_general(a, b, (((0,), (0,)), ((), ())), preferred_element_type=F32)


def centred_of(tokens):
    values = tokens.astype(F32)
    centred = values - jnp.mean(values, axis=-1, keepdims=True)
    spread = jnp.mean(centred * centred, axis=-1, keepdims=True)
    return centred, lax.rsqrt(spread + epsilon)


def chunk_rows(ch):
    return pl.ds(pl.multiple_of(ch * TOK, TOK), TOK)


def normalise(ch, tokens, cots, shift, scale, normed, cot):
    def group(g):
        centred, rate = centred_of(tokens[ch, pl.ds(g * GROUP, GROUP)].astype(F32).reshape(GROUP * CP, D))
        here = pl.ds(pl.multiple_of(ch * TOK + g * GROUP * CP, GROUP * CP), GROUP * CP)
        normed[here, :] = (centred * rate * (1.0 + scale[...]) + shift[...]).astype(BF16)
        here = pl.ds(pl.multiple_of(g * GROUP * CP, GROUP * CP), GROUP * CP)
        pair = cots[lax.div(ch, 2), pl.ds(g * GROUP, GROUP)].astype(F32).reshape(GROUP * CP, 2 * INNER)
        cot[here, :INNER] = jnp.where(lax.rem(ch, 2) == 0, pair[:, :INNER], pair[:, INNER:]).astype(BF16)

    loop(0, SEQ // GROUP, group)


def attention(ch, w, proj, gproj, normed, cot, block):
    rows = chunk_rows(ch)
    for i in range(3):
        proj[i] = jnp.dot(normed[rows, :], w[i], preferred_element_type=F32).astype(BF16)
    factor = HD ** (-0.5)
    lane = lax.broadcasted_iota(jnp.int32, (TOK, 256), 1)
    upper = [None] * 3
    for a in range(4):
        lanes = pl.ds(128 * a, 256)
        masks = []
        for t in range(2):
            low = 16 * a + HD * t
            masks.append(jnp.where((lane >= low) & (lane < low + HD), 1.0, 0.0).astype(BF16))

        def two(values):
            return jnp.concatenate([values * mask for mask in masks], axis=0)

        key, value = proj[1, :, lanes], proj[2, :, lanes]
        queries, keys, grads = two(proj[0, :, lanes]), two(key), two(cot[:, lanes])
        scores = dot_last(queries, key) * factor + block[...]
        expo = jnp.exp(scores - jnp.max(scores, axis=-1, keepdims=True))
        attend = expo / jnp.sum(expo, axis=-1, keepdims=True)
        dots = dot_last(grads, value)
        gscores = attend * (dots - jnp.sum(attend * dots, axis=-1, keepdims=True)) * factor
        gscores = gscores.astype(BF16)
        side = jnp.concatenate([gscores[:TOK], gscores[TOK:]], axis=1)
        found = (
            jnp.dot(side, keys, preferred_element_type=F32),
            dot_first(gscores, queries),
            dot_first(attend.astype(BF16), grads),
        )
        for i in range(3):
            lower = found[i][:, :128] if a == 0 else found[i][:, :128] + upper[i]
            gproj[i, rows, pl.ds(128 * a, 128)] = lower.astype(BF16)
            upper[i] = found[i][:, 128:]
    for i in range(3):
        gproj[i, rows, pl.ds(512, 128)] = upper[i].astype(BF16)


def grad_normed(ch, w, gproj, gnorm):
    rows = chunk_rows(ch)

    def part(n):
        cut = pl.ds(pl.multiple_of(n * 384, 128), 384)
        total = dot_last(gproj[0, rows, :], w[0, cut, :])
        total += dot_last(gproj[1, rows, :], w[1, cut, :])
        total += dot_last(gproj[2, rows, :], w[2, cut, :])
        gnorm[:, cut] = total

    loop(0, 3, part)


def grad_tokens(ch, g, tokens, away, scale, gnorm):
    frames = pl.ds(g * GROUP, GROUP)
    centred, rate = centred_of(tokens[ch, frames].astype(F32).reshape(GROUP * CP, D))
    unit = centred * rate
    grad = gnorm[pl.ds(pl.multiple_of(g * GROUP * CP, GROUP * CP), GROUP * CP), :] * (1.0 + scale[...])
    mean = jnp.mean(grad, axis=-1, keepdims=True)
    along = jnp.mean(grad * unit, axis=-1, keepdims=True)
    away[ch, frames] = (rate * (grad - mean - unit * along)).reshape(GROUP, CP, D).astype(BF16)


def weight_partial(first, count, normed, gproj, gw):
    rows = pl.ds(first * TOK, count * TOK)

    def part(n):
        cut = pl.ds(pl.multiple_of(n * 384, 128), 384)
        for i in range(3):
            term = dot_first(normed[rows, cut], gproj[i, rows, :])
            if first == 0:
                gw[i, cut, :] = term
            else:
                gw[i, cut, :] += term

    loop(0, 3, part)


def narrow(parts):
    return jnp.concatenate([part[:, :INNER] for part in parts], axis=1)


def kernel(
    x, cot_in, shift, scale, w_in, out, gout,
    rows_in, turned, paired, wp, tiles, tokens, cots, away, proj, gproj, normed, cot, gnorm, block, w, gw,
    g1, g2, g3, far, near, half, a1, a2, b1, b2, fours, column,
    sx, rx, sc, rc, sb, rb, own_sems,
    gzs, gzr, gps, gpr, gcs, gcr, rcs, rcr, rps, rpr, rzs, rzr, rss, rsr,
):
    spot = place()
    s, d, z, c, hi, q = spot
    weight = Gather((wp, w, g1, g2, g3, gzs, gzr, gps, gpr, gcs, gcr, own_sems.at[0]), spot)
    total = Reduce(
        (gw, tiles, far, near, half, a1, a2, b1, b2, fours, column, rcs, rcr, rps, rpr, rzs, rzr, rss, rsr), spot
    )
    for i in range(1, SEQ):
        greet(wrap(s + i), d)
    for i in range(1, NXY):
        greet(s, hi * NXY + wrap(q + i))
    for at in (z, lax.rem(z + 4, NZ)):
        greet(2 * at + c, (1 - hi) * NXY + q)

    def group_of(j, ch):
        return j * CH + ch

    def send_x(ch, i):
        j = wrap(s + i)
        return remote(x.at[group_of(j, ch)], tokens.at[ch, s], sx.at[ch, i - 1], rx.at[ch, i - 1], j, d)

    def send_c(pair, i):
        j = wrap(s + i)
        return remote(paired.at[j, pair], cots.at[pair, s], sc.at[pair, i - 1], rc.at[pair, i - 1], j, d)

    def send_back(ch, i):
        j = wrap(s + i)
        return remote(away.at[ch, j], out.at[group_of(s, ch)], sb.at[ch, i - 1], rb.at[ch, i - 1], j, d)

    def keep_back(ch):
        return pltpu.make_async_copy(away.at[ch, s], out.at[group_of(s, ch)], own_sems.at[1 + ch])

    def sent_all(copy, k):
        for i in range(1, SEQ):
            copy(k, i).wait_send()

    def came_all(copy, k):
        for i in range(1, SEQ):
            copy(k, i).wait_recv()

    order = ((send_x, 0), (send_c, 0), (send_x, 1), (send_x, 2), (send_c, 1), (send_x, 3))

    def feed(first, last):
        for k, (copy, which) in enumerate(order):
            low, high = max(first - 15 * k, 0), min(last - 15 * k, 15)
            if low < high:
                for i in range(low + 1, high + 1):
                    copy(which, 7 * i % SEQ).start()

    def give_back(first, last):
        for n in range(first, last):
            send_back(n // 15, n % 15 + 1).start()

    load = pltpu.make_async_copy(w_in, rows_in, own_sems.at[0])
    turn = pltpu.make_async_copy(cot_in, turned, own_sems.at[1 + CH])
    load.start()
    turn.start()
    keeps = []
    for ch in range(CH):
        keeps.append(pltpu.make_async_copy(x.at[group_of(s, ch)], tokens.at[ch, s], own_sems.at[1 + ch]))
    for keep in keeps:
        keep.start()
    load.wait()
    pl.semaphore_wait(pltpu.get_barrier_semaphore(), SEQ - 1 + NXY - 1 + 2)

    gap = jnp.zeros((ROWS, WIDE - INNER), F32)
    for i in range(3):
        part = rows_in[:, pl.ds(i * INNER, INNER)].astype(F32)
        part = jnp.concatenate([part, gap], axis=1).astype(BF16)
        for t in range(5):
            wp[5 * i + t] = part[:, 128 * t : 128 * t + 128]
    wp[15] = jnp.zeros((ROWS, 128), BF16)
    weight.begin()

    def pair_up(b):
        values = turned[:, pl.ds(pl.multiple_of(b * 128, 128), 128)].astype(F32).T
        values = values.reshape(4, 2, 2, CP, INNER)
        sides = jnp.concatenate([values[:, :, 0], values[:, :, 1]], axis=-1)
        paired[pl.ds(4 * b, 4)] = sides.astype(BF16)

    def between(step):
        feed(FEEDS[step + 2], FEEDS[step + 3])
        if step == -2:
            turn.wait()
            loop(0, 2, pair_up)
        if step == -1:
            loop(2, 4, pair_up)
            for pair in range(CH // 2):
                keeps.append(
                    pltpu.make_async_copy(paired.at[s, pair], cots.at[pair, s], own_sems.at[1 + CH + pair])
                )
                keeps[-1].start()
        if step == 0:
            row = lax.broadcasted_iota(jnp.int32, (2 * TOK, TOK), 0)
            column_of = lax.broadcasted_iota(jnp.int32, (2 * TOK, TOK), 1)
            block[...] = jnp.where(lax.rem(row, CP) == lax.rem(column_of, CP), 0.0, -1e30)
            cot[:, pl.ds(512, 128)] = jnp.zeros((TOK, 128), BF16)
            for keep in keeps:
                keep.wait()

    weight.collect(between)
    feed(FEEDS[7], 90)

    def forward(ch):
        came_all(send_x, ch)

        @pl.when(lax.rem(ch, 2) == 0)
        def _():
            came_all(send_c, lax.div(ch, 2))

        normalise(ch, tokens, cots, shift, scale, normed, cot)
        attention(ch, w, proj, gproj, normed, cot, block)

    def backward(ch):
        grad_normed(ch, w, gproj, gnorm)
        loop(0, SEQ // GROUP, lambda g: grad_tokens(ch, g, tokens, away, scale, gnorm))

    def early(ch):
        forward(ch)

        @pl.when(ch < 2)
        def _():
            backward(ch)
            keep_back(ch).start()

        @pl.when(ch == 1)
        def _():
            weight_partial(0, 2, normed, gproj, gw)

    loop(0, 3, early)
    weight_partial(2, 1, normed, gproj, gw)
    sent_all(send_x, 3)
    counts, started = iter(RETURNS), [0]

    def beside():
        first = started[0]
        started[0] = min(first + next(counts), 60)
        give_back(first, started[0])

    beside()
    forward(3)
    beside()
    weight_partial(3, 1, normed, gproj, gw)
    beside()
    total.begin(beside)

    def last_chunk():
        for ch in (2, 3):
            backward(ch)
            keep_back(ch).start()

    def returned(ch):
        for i in range(1, SEQ):
            send_back(ch, i).wait()
        keep_back(ch).wait()

    def settle():
        weight.finish()
        for pair in range(CH // 2):
            sent_all(send_c, pair)
        for ch in range(CH - 1):
            sent_all(send_x, ch)
        total.finish()
        for ch in range(CH - 1):
            returned(ch)

    total.sum_up(beside, last_chunk, settle)
    gout[...] = narrow([jnp.concatenate([tiles[5 * i + t].astype(F32) for t in range(5)], axis=1) for i in range(3)]).astype(
        BF16
    )
    returned(CH - 1)


FEEDS = (0, 8, 14, 20, 26, 38, 46, 52)
RETURNS = (10, 6, 6) + (0,) * 16 + (6, 6, 3, 2, 3, 3, 60)


def fused(x, cot, shift, scale, w):
    vm, hbm = pl.BlockSpec(memory_space=pltpu.VMEM), pl.BlockSpec(memory_space=pl.ANY)
    dma = pltpu.SemaphoreType.DMA
    return pl.pallas_call(
        kernel,
        out_shape=(jax.ShapeDtypeStruct(x.shape, BF16), jax.ShapeDtypeStruct((ROWS, 3 * INNER), BF16)),
        in_specs=[hbm, hbm, vm, vm, hbm],
        out_specs=(vm, vm),
        scratch_shapes=[
            pltpu.VMEM((ROWS, 3 * INNER), BF16),
            pltpu.VMEM((INNER, PATCH), BF16),
            pltpu.VMEM((SEQ, CH // 2, CP, 2 * INNER), BF16),
            pltpu.VMEM((NQ, ROWS, 128), BF16),
            pltpu.VMEM((NQ, ROWS, 128), BF16),
            pltpu.VMEM((CH, SEQ, CP, D), BF16),
            pltpu.VMEM((CH // 2, SEQ, CP, 2 * INNER), BF16),
            pltpu.VMEM((CH, SEQ, CP, D), BF16),
            pltpu.VMEM((3, TOK, WIDE), BF16),
            pltpu.VMEM((3, CH * TOK, WIDE), BF16),
            pltpu.VMEM((CH * TOK, D), BF16),
            pltpu.VMEM((TOK, WIDE), BF16),
            pltpu.VMEM((TOK, D), F32),
            pltpu.VMEM((2 * TOK, TOK), F32),
            pltpu.VMEM((3, D, WIDE), BF16),
            pltpu.VMEM((3, D, WIDE), F32),
            pltpu.VMEM((2, 4, ROWS, 128), BF16),
            pltpu.VMEM((4, 4, 2, 4, ROWS, 128), BF16),
            pltpu.VMEM((4, 4, 2, 4, ROWS, 128), BF16),
            pltpu.VMEM((4, 4, 2, 4, ROWS, 128), BF16),
            pltpu.VMEM((4, 4, 2, 4, ROWS, 128), BF16),
            pltpu.VMEM((4, 4, 2, 4, ROWS, 128), BF16),
            pltpu.VMEM((2, 2, 4, 2, ROWS, 128), BF16),
            pltpu.VMEM((2, 2, 4, 4, ROWS, 128), BF16),
            pltpu.VMEM((2, 2, 2, ROWS, 128), BF16),
            pltpu.VMEM((2, 2, 4, ROWS, 128), BF16),
            pltpu.VMEM((3, 2, ROWS, 128), BF16),
            pltpu.VMEM((3, ROWS, 128), BF16),
        ]
        + [dma((CH, SEQ - 1))] * 2
        + [dma((CH // 2, SEQ - 1))] * 2
        + [dma((CH, SEQ - 1))] * 2
        + [
            dma((1 + 2 * CH,)),
            dma((4,)),
            dma((4,)),
            dma((2, 4, 2)),
            dma((2, 4, 2)),
            dma((2, 7)),
            dma((2, 7)),
            dma((2, 4)),
            dma((2, 4)),
            dma((2, 6, 2)),
            dma((2, 6, 2)),
            dma((6,)),
            dma((6,)),
            dma((NXY - 1,)),
            dma((NXY - 1,)),
        ],
        compiler_params=pltpu.CompilerParams(
            collective_id=0, has_side_effects=True, vmem_limit_bytes=60 * 1024 * 1024
        ),
        name="temporal_backward",
    )(x, cot, shift, scale, w)


def body(frames, shift_table, scale_table, grad_attended, w_qkv):
    x = frames.reshape(SEQ * CH, CP, D)
    cot = grad_attended[0, 0].T
    grad_tokens, grad_weight = fused(x, cot, shift_table, scale_table, w_qkv)
    return grad_tokens.reshape(frames.shape), grad_weight


def solution(mesh):
    placed = (
        P("dp", "seq", None, None),
        P("dp", None),
        P("dp", None),
        P("dp", "seq", None, None),
        P("seq", None),
    )
    return jax.shard_map(
        body,
        mesh=mesh,
        in_specs=placed,
        out_specs=(P("dp", "seq", None, None), P("seq", None)),
        check_vma=False,
    )
```

```python
import jax
import jax.numpy as jnp
from jax import lax
from jax.experimental import pallas as pl
from jax.experimental.pallas import tpu as pltpu
from jax.sharding import PartitionSpec as P

MESH = pl.DeviceIdType.MESH
F32 = jnp.float32
BF16 = jnp.bfloat16

D = 1152
HD = 72
INNER = 576
WIDE = 640
SEQ = 16
NZ = 8
NXY = 16
NQ = 16
ROWS = 72
PATCH = 512
OWN = 32
CH = 4
CP = 8
GROUP = 4
TOK = SEQ * CP
epsilon = 1e-06


def place():
    s, d = lax.axis_index("seq"), lax.axis_index("dp")
    return s, d, lax.div(s, 2), lax.rem(s, 2), lax.div(d, NXY), lax.rem(d, NXY)


def remote(src, dst, send, recv, seq, dp):
    return pltpu.make_async_remote_copy(
        src_ref=src,
        dst_ref=dst,
        send_sem=send,
        recv_sem=recv,
        device_id={"seq": seq, "dp": dp},
        device_id_type=MESH,
    )


def loop(start, stop, body):
    def step(i, carry):
        body(i)
        return carry

    lax.fori_loop(start, stop, step, 0)


def wrap(place):
    return jnp.where(place >= 16, place - 16, place)


def greet(seq, dp):
    pl.semaphore_signal(
        pltpu.get_barrier_semaphore(),
        inc=1,
        device_id={"seq": seq, "dp": dp},
        device_id_type=MESH,
    )


def neighbours(me):
    return lax.rem(me + 1, 4), lax.rem(me + 3, 4), lax.rem(me + 2, 4)


def plane_device(h, stage, step, hi, x, y):
    along_x = (h == 0) == (stage == 0)
    me = x if along_x else y
    to = neighbours(me)[step]
    return hi * NXY + (to * 4 + y if along_x else x * 4 + to)


class Gather:
    def __init__(self, refs, spot):
        self.wp, self.w, self.g1, self.g2, self.g3, self.zs, self.zr, self.ps, self.pr, self.cs, self.cr, self.own = refs
        self.spot = spot

    def along_z(self, i):
        s, d, z, c, hi, q = self.spot
        four, at = lax.div(z, 4), lax.rem(z, 4)
        if isinstance(i, int) and i == 0:
            to = 2 * (4 * (1 - four) + at) + c
            return remote(self.wp.at[q], self.g1.at[four, at], self.zs.at[0], self.zr.at[0], to, d)
        to = 2 * (4 * four + lax.rem(at + i, 4)) + c
        return remote(self.g1.at[:, at], self.g1.at[:, at], self.zs.at[i], self.zr.at[i], to, d)

    def plane(self, h, step, way):
        s, d, z, c, hi, q = self.spot
        x, y = lax.div(q, 4), lax.rem(q, 4)
        stage, passes = step // 2, step % 2
        rows = pl.ds(2 * way, 2) if passes else slice(None)
        axis_x = (h == 0) == (stage == 0)
        other = neighbours(x if axis_x else y)[1 - way]
        if stage == 0:
            px, py = x, y
            if passes:
                px, py = (other, y) if axis_x else (x, other)
            piece = self.g2.at[px, py, h, rows]
        else:
            line = other if passes else (x if axis_x else y)
            piece = self.g2.at[line, :, h, rows] if axis_x else self.g2.at[:, line, h, rows]
        to = plane_device(h, stage, way, hi, x, y)
        return remote(piece, piece, self.ps.at[h, step, way], self.pr.at[h, step, way], s, to)

    def across(self, h, k):
        s, d, z, c, hi, q = self.spot
        x, y = lax.div(q, 4), lax.rem(q, 4)
        stage, which = k // 3, k % 3
        axis_x = (h == 0) == (stage == 0)
        other = neighbours(x if axis_x else y)[which]

        def region(ref):
            if stage == 0:
                return ref.at[other, y, h] if axis_x else ref.at[x, other, h]
            return ref.at[other, :, h] if axis_x else ref.at[:, other, h]

        return remote(
            region(self.g2), region(self.g3), self.cs.at[h, k], self.cr.at[h, k], 2 * z + 1 - c, d
        )

    def own_across(self):
        s, d, z, c, hi, q = self.spot
        x, y = lax.div(q, 4), lax.rem(q, 4)
        return remote(self.g2.at[x, y], self.g3.at[x, y], self.cs.at[0, 6], self.cr.at[0, 6], 2 * z + 1 - c, d)

    def begin(self):
        self.along_z(0).start()

    def collect(self, between):
        s, d, z, c, hi, q = self.spot
        x, y = lax.div(q, 4), lax.rem(q, 4)
        own = pltpu.make_async_copy(self.wp.at[q], self.g1.at[lax.div(z, 4), lax.rem(z, 4)], self.own)
        own.start()
        own.wait()
        between(-2)
        self.along_z(0).wait_recv()
        loop(1, 4, lambda i: self.along_z(i).start())
        between(-1)
        loop(1, 4, lambda i: self.along_z(i).wait_recv())
        own = pltpu.make_async_copy(self.g1, self.g2.at[x, y], self.own)
        own.start()
        own.wait()
        for step in range(4):
            for h in range(2):
                if step:
                    for way in range(2):
                        self.plane(h, step - 1, way).wait_recv()
                for way in range(2):
                    self.plane(h, step, way).start()
                if step == 0 and h == 0:
                    self.own_across().start()
                if step % 2:
                    for k in range(2):
                        self.across(h, 3 * (step // 2) + k).start()
                elif step:
                    self.across(h, 2).start()
            between(step)
        for h in range(2):
            for way in range(2):
                self.plane(h, 3, way).wait_recv()
            self.across(h, 5).start()
        between(4)
        self.own_across().wait_recv()
        for h in range(2):
            for k in range(6):
                self.across(h, k).wait_recv()

        def assemble(t):
            piece, row = lax.div(t, NZ), lax.rem(t, NZ)
            part, tile = lax.div(piece, 5), lax.rem(piece, 5)
            px, py = lax.div(piece, 4), lax.rem(piece, 4)
            here = self.g2[px, py, lax.div(row, 4), lax.rem(row, 4)].astype(F32)
            there = self.g3[px, py, lax.div(row, 4), lax.rem(row, 4)].astype(F32)
            both = jnp.concatenate([jnp.where(c == 0, here, there), jnp.where(c == 0, there, here)], axis=0)
            lanes = pl.ds(pl.multiple_of(tile * 128, 128), 128)
            self.w[part, pl.ds(pl.multiple_of(row * 144, 16), 144), lanes] = both.astype(BF16)

        loop(0, 15 * NZ, assemble)

    def finish(self):
        for i in range(4):
            self.along_z(i).wait_send()
        self.own_across().wait_send()
        for h in range(2):
            for step in range(4):
                for way in range(2):
                    self.plane(h, step, way).wait_send()
            for k in range(6):
                self.across(h, k).wait_send()


class Reduce:
    def __init__(self, refs, spot):
        (self.gw, self.out, self.away, self.near, self.half, self.a1, self.a2, self.b1, self.b2, self.fours, self.column) = refs[:11]
        (self.cs, self.cr, self.ps, self.pr, self.zs, self.zr, self.ss, self.sr) = refs[11:]
        self.spot = spot

    def block(self, piece, row, core):
        part, tile = lax.div(piece, 5), lax.rem(piece, 5)
        first = pl.multiple_of(row * 144 + core * ROWS, 8)
        return self.gw[part, pl.ds(first, ROWS), pl.ds(pl.multiple_of(tile * 128, 128), 128)]

    def lines(self, h, stage=0):
        q = self.spot[5]
        axis_x = (h == 0) == (stage == 0)
        me = lax.div(q, 4) if axis_x else lax.rem(q, 4)
        plus, minus, opposite = neighbours(me)
        return (opposite, plus, minus, me), axis_x

    def across(self, h, k):
        s, d, z, c, hi, q = self.spot
        places, axis_x = self.lines(h)

        def line(ref):
            return ref.at[places[k], :, h] if axis_x else ref.at[:, places[k], h]

        return remote(line(self.away), line(self.near), self.cs.at[h, k], self.cr.at[h, k], 2 * z + 1 - c, d)

    def each(self, h, k, body):
        places, axis_x = self.lines(h)

        def one(t):
            a, r = lax.div(t, 4), lax.rem(t, 4)
            px, py = (places[k], a) if axis_x else (a, places[k])
            body((px, py, h, r), jnp.minimum(4 * px + py, 14), 4 * h + r)

        loop(0, 16, one)

    def give(self, h, k):
        c = self.spot[3]

        def fill(at, piece, row):
            self.away[at] = self.block(piece, row, 1 - c).astype(BF16)

        self.each(h, k, fill)
        self.across(h, k).start()

    def take(self, h, k):
        c = self.spot[3]
        self.across(h, k).wait_recv()

        def fill(at, piece, row):
            self.half[at] = (self.block(piece, row, c) + self.near[at].astype(F32)).astype(BF16)

        self.each(h, k, fill)

    def plane(self, h, stage, part, way):
        s, d, z, c, hi, q = self.spot
        x, y = lax.div(q, 4), lax.rem(q, 4)
        places, axis_x = self.lines(h, stage)
        place = places[0] if part == 0 else places[1 + way]
        rows = pl.ds(2 * (1 - way) if part == 1 else 2 * way, 2)
        if stage == 0:
            piece = self.half.at[place, :, h, rows] if axis_x else self.half.at[:, place, h, rows]
            landing = self.a1.at[h, way] if part == 0 else self.a2.at[h, way, :, rows]
        else:
            piece = self.half.at[place, y, h, rows] if axis_x else self.half.at[x, place, h, rows]
            landing = self.b1.at[h, way] if part == 0 else self.b2.at[h, way, rows]
        at = (h, 3 * stage + part, way)
        return remote(piece, landing, self.ps.at[at], self.pr.at[at], s, plane_device(h, stage, way, hi, x, y))

    def add(self, h, stage, last):
        q = self.spot[5]
        x, y = lax.div(q, 4), lax.rem(q, 4)
        places, axis_x = self.lines(h, stage)

        def spot_of(place, a, row):
            if stage == 0:
                return (place, a, h, row) if axis_x else (a, place, h, row)
            return (place, y, h, row) if axis_x else (x, place, h, row)

        def one(t):
            if last:
                a, r = lax.div(t, 4), lax.rem(t, 4)
                at = spot_of(places[3], a, r)
                total = self.half[at].astype(F32)
                for way in range(2):
                    total += (self.a2[h, way, a, r] if stage == 0 else self.b2[h, way, r]).astype(F32)
                self.half[at] = total.astype(BF16)
            else:
                a, r = lax.div(t, 2), lax.rem(t, 2)
                for way in range(2):
                    at = spot_of(places[1 + way], a, 2 * way + r)
                    here = self.a1[h, way, a, r] if stage == 0 else self.b1[h, way, r]
                    self.half[at] = (self.half[at].astype(F32) + here.astype(F32)).astype(BF16)

        loop(0, (4 if stage == 0 else 1) * (4 if last else 2), one)

    def begin(self, beside):
        for k in range(4):
            for h in range(2):
                self.give(h, k)
                beside()

    def in_four(self, i):
        s, d, z, c, hi, q = self.spot
        there = lax.rem(lax.rem(z, 4) + i, 4)
        source = self.half.at[lax.div(q, 4), lax.rem(q, 4), :, there]
        to = 2 * (4 * lax.div(z, 4) + there) + c
        return remote(source, self.fours.at[i - 1], self.zs.at[i - 1], self.zr.at[i - 1], to, d)

    def far_off(self, k):
        s, d, z, c, hi, q = self.spot
        four, at = lax.div(z, 4), lax.rem(z, 4)
        block = four if k == 2 else 1 - four
        source = self.half.at[lax.div(q, 4), lax.rem(q, 4), block, at]
        to = 2 * (4 * block + at) + c
        dp = d if k == 0 else (1 - hi) * NXY + q
        return remote(source, self.column.at[k], self.zs.at[3 + k], self.zr.at[3 + k], to, dp)

    def spread(self, i):
        s, d, z, c, hi, q = self.spot
        to = hi * NXY + wrap(q + i)
        return remote(self.out.at[q], self.out.at[q], self.ss.at[i - 1], self.sr.at[i - 1], s, to)

    def sum_up(self, beside, between, settle):
        s, d, z, c, hi, q = self.spot
        ways = [(h, way) for h in range(2) for way in range(2)]
        for stage in range(2):
            for part in range(2):
                for h in range(2):
                    if stage == 0:
                        for k in (0,) if part == 0 else (1, 2):
                            self.take(h, k)
                            beside()
                    for way in range(2):
                        self.plane(h, stage, part, way).start()
            if stage == 0:
                for h in range(2):
                    self.take(h, 3)
                    beside()
                between()
            beside()
            for h in range(2):
                for way in range(2):
                    self.plane(h, stage, 0, way).wait_recv()
                self.add(h, stage, False)
                for way in range(2):
                    self.plane(h, stage, 2, way).start()
            beside()
            for h in range(2):
                for way in range(2):
                    for part in (1, 2):
                        self.plane(h, stage, part, way).wait_recv()
                self.add(h, stage, True)
        px, py, four, at = lax.div(q, 4), lax.rem(q, 4), lax.div(z, 4), lax.rem(z, 4)
        loop(1, 4, lambda i: self.in_four(i).start())
        beside()
        loop(1, 4, lambda i: self.in_four(i).wait_recv())
        for block in range(2):
            total = self.half[px, py, block, at].astype(F32)
            for i in range(3):
                total += self.fours[i, block].astype(F32)
            self.half[px, py, block, at] = total.astype(BF16)
        for k in range(3):
            self.far_off(k).start()
        beside()
        for k in range(3):
            self.far_off(k).wait_recv()
        total = self.half[px, py, four, at].astype(F32)
        for k in range(3):
            total += self.column[k].astype(F32)
        self.out[q] = total.astype(BF16)
        for i in range(1, NXY):
            self.spread(i).start()
        beside()
        settle()
        for i in range(1, NXY):
            self.spread(i).wait()

    def finish(self):
        for h in range(2):
            for k in range(4):
                self.across(h, k).wait_send()
            for stage in range(2):
                for part in range(3):
                    for way in range(2):
                        self.plane(h, stage, part, way).wait_send()
        loop(1, 4, lambda i: self.in_four(i).wait_send())
        for k in range(3):
            self.far_off(k).wait_send()


def dot_last(a, b):
    return lax.dot_general(a, b, (((1,), (1,)), ((), ())), preferred_element_type=F32)


def dot_first(a, b):
    return lax.dot_general(a, b, (((0,), (0,)), ((), ())), preferred_element_type=F32)


def centred_of(tokens):
    values = tokens.astype(F32)
    centred = values - jnp.mean(values, axis=-1, keepdims=True)
    spread = jnp.mean(centred * centred, axis=-1, keepdims=True)
    return centred, lax.rsqrt(spread + epsilon)


def chunk_rows(ch):
    return pl.ds(pl.multiple_of(ch * TOK, TOK), TOK)


def normalise(ch, tokens, cots, shift, scale, normed, cot):
    def group(g):
        centred, rate = centred_of(tokens[ch, pl.ds(g * GROUP, GROUP)].astype(F32).reshape(GROUP * CP, D))
        here = pl.ds(pl.multiple_of(ch * TOK + g * GROUP * CP, GROUP * CP), GROUP * CP)
        normed[here, :] = (centred * rate * (1.0 + scale[...]) + shift[...]).astype(BF16)
        here = pl.ds(pl.multiple_of(g * GROUP * CP, GROUP * CP), GROUP * CP)
        pair = cots[lax.div(ch, 2), pl.ds(g * GROUP, GROUP)].astype(F32).reshape(GROUP * CP, 2 * INNER)
        cot[here, :INNER] = jnp.where(lax.rem(ch, 2) == 0, pair[:, :INNER], pair[:, INNER:]).astype(BF16)

    loop(0, SEQ // GROUP, group)


def attention(ch, w, proj, gproj, normed, cot, block):
    rows = chunk_rows(ch)
    for i in range(3):
        proj[i] = jnp.dot(normed[rows, :], w[i], preferred_element_type=F32).astype(BF16)
    factor = HD ** (-0.5)
    lane = lax.broadcasted_iota(jnp.int32, (TOK, 256), 1)
    upper = [None] * 3
    for a in range(4):
        lanes = pl.ds(128 * a, 256)
        masks = []
        for t in range(2):
            low = 16 * a + HD * t
            masks.append(jnp.where((lane >= low) & (lane < low + HD), 1.0, 0.0).astype(BF16))

        def two(values):
            return jnp.concatenate([values * mask for mask in masks], axis=0)

        key, value = proj[1, :, lanes], proj[2, :, lanes]
        queries, keys, grads = two(proj[0, :, lanes]), two(key), two(cot[:, lanes])
        scores = dot_last(queries, key) * factor + block[...]
        expo = jnp.exp(scores - jnp.max(scores, axis=-1, keepdims=True))
        attend = expo / jnp.sum(expo, axis=-1, keepdims=True)
        dots = dot_last(grads, value)
        gscores = attend * (dots - jnp.sum(attend * dots, axis=-1, keepdims=True)) * factor
        gscores = gscores.astype(BF16)
        side = jnp.concatenate([gscores[:TOK], gscores[TOK:]], axis=1)
        found = (
            jnp.dot(side, keys, preferred_element_type=F32),
            dot_first(gscores, queries),
            dot_first(attend.astype(BF16), grads),
        )
        for i in range(3):
            lower = found[i][:, :128] if a == 0 else found[i][:, :128] + upper[i]
            gproj[i, rows, pl.ds(128 * a, 128)] = lower.astype(BF16)
            upper[i] = found[i][:, 128:]
    for i in range(3):
        gproj[i, rows, pl.ds(512, 128)] = upper[i].astype(BF16)


def grad_normed(ch, w, gproj, gnorm):
    rows = chunk_rows(ch)

    def part(n):
        cut = pl.ds(pl.multiple_of(n * 384, 128), 384)
        total = dot_last(gproj[0, rows, :], w[0, cut, :])
        total += dot_last(gproj[1, rows, :], w[1, cut, :])
        total += dot_last(gproj[2, rows, :], w[2, cut, :])
        gnorm[:, cut] = total

    loop(0, 3, part)


def grad_tokens(ch, g, tokens, away, scale, gnorm):
    frames = pl.ds(g * GROUP, GROUP)
    centred, rate = centred_of(tokens[ch, frames].astype(F32).reshape(GROUP * CP, D))
    unit = centred * rate
    grad = gnorm[pl.ds(pl.multiple_of(g * GROUP * CP, GROUP * CP), GROUP * CP), :] * (1.0 + scale[...])
    mean = jnp.mean(grad, axis=-1, keepdims=True)
    along = jnp.mean(grad * unit, axis=-1, keepdims=True)
    away[ch, frames] = (rate * (grad - mean - unit * along)).reshape(GROUP, CP, D).astype(BF16)


def weight_partial(first, count, normed, gproj, gw):
    rows = pl.ds(first * TOK, count * TOK)

    def part(n):
        cut = pl.ds(pl.multiple_of(n * 384, 128), 384)
        for i in range(3):
            term = dot_first(normed[rows, cut], gproj[i, rows, :])
            if first == 0:
                gw[i, cut, :] = term
            else:
                gw[i, cut, :] += term

    loop(0, 3, part)


def narrow(parts):
    return jnp.concatenate([part[:, :INNER] for part in parts], axis=1)


def kernel(
    x, cot_in, shift, scale, w_in, out, gout,
    rows_in, turned, paired, wp, tiles, tokens, cots, away, proj, gproj, normed, cot, gnorm, block, w, gw,
    g1, g2, g3, far, near, half, a1, a2, b1, b2, fours, column,
    sx, rx, sc, rc, sb, rb, own_sems,
    gzs, gzr, gps, gpr, gcs, gcr, rcs, rcr, rps, rpr, rzs, rzr, rss, rsr,
):
    spot = place()
    s, d, z, c, hi, q = spot
    weight = Gather((wp, w, g1, g2, g3, gzs, gzr, gps, gpr, gcs, gcr, own_sems.at[0]), spot)
    total = Reduce(
        (gw, tiles, far, near, half, a1, a2, b1, b2, fours, column, rcs, rcr, rps, rpr, rzs, rzr, rss, rsr), spot
    )
    for i in range(1, SEQ):
        greet(wrap(s + i), d)
    for i in range(1, NXY):
        greet(s, hi * NXY + wrap(q + i))
    for at in (z, lax.rem(z + 4, NZ)):
        greet(2 * at + c, (1 - hi) * NXY + q)

    def group_of(j, ch):
        return j * CH + ch

    def send_x(ch, i):
        j = wrap(s + i)
        return remote(x.at[group_of(j, ch)], tokens.at[ch, s], sx.at[ch, i - 1], rx.at[ch, i - 1], j, d)

    def send_c(pair, i):
        j = wrap(s + i)
        return remote(paired.at[j, pair], cots.at[pair, s], sc.at[pair, i - 1], rc.at[pair, i - 1], j, d)

    def send_back(ch, i):
        j = wrap(s + i)
        return remote(away.at[ch, j], out.at[group_of(s, ch)], sb.at[ch, i - 1], rb.at[ch, i - 1], j, d)

    def keep_back(ch):
        return pltpu.make_async_copy(away.at[ch, s], out.at[group_of(s, ch)], own_sems.at[1 + ch])

    def sent_all(copy, k):
        for i in range(1, SEQ):
            copy(k, i).wait_send()

    def came_all(copy, k):
        for i in range(1, SEQ):
            copy(k, i).wait_recv()

    order = ((send_x, 0), (send_c, 0), (send_x, 1), (send_x, 2), (send_c, 1), (send_x, 3))

    def feed(first, last):
        for k, (copy, which) in enumerate(order):
            low, high = max(first - 15 * k, 0), min(last - 15 * k, 15)
            if low < high:
                for i in range(low + 1, high + 1):
                    copy(which, 7 * i % SEQ).start()

    def give_back(first, last):
        for n in range(first, last):
            send_back(n // 15, n % 15 + 1).start()

    load = pltpu.make_async_copy(w_in, rows_in, own_sems.at[0])
    turn = pltpu.make_async_copy(cot_in, turned, own_sems.at[1 + CH])
    load.start()
    turn.start()
    keeps = []
    for ch in range(CH):
        keeps.append(pltpu.make_async_copy(x.at[group_of(s, ch)], tokens.at[ch, s], own_sems.at[1 + ch]))
    for keep in keeps:
        keep.start()
    load.wait()
    pl.semaphore_wait(pltpu.get_barrier_semaphore(), SEQ - 1 + NXY - 1 + 2)

    gap = jnp.zeros((ROWS, WIDE - INNER), F32)
    for i in range(3):
        part = rows_in[:, pl.ds(i * INNER, INNER)].astype(F32)
        part = jnp.concatenate([part, gap], axis=1).astype(BF16)
        for t in range(5):
            wp[5 * i + t] = part[:, 128 * t : 128 * t + 128]
    wp[15] = jnp.zeros((ROWS, 128), BF16)
    weight.begin()

    def pair_up(b):
        values = turned[:, pl.ds(pl.multiple_of(b * 128, 128), 128)].astype(F32).T
        values = values.reshape(4, 2, 2, CP, INNER)
        sides = jnp.concatenate([values[:, :, 0], values[:, :, 1]], axis=-1)
        paired[pl.ds(4 * b, 4)] = sides.astype(BF16)

    def between(step):
        feed(FEEDS[step + 2], FEEDS[step + 3])
        if step == -2:
            turn.wait()
            loop(0, 2, pair_up)
        if step == -1:
            loop(2, 4, pair_up)
            for pair in range(CH // 2):
                keeps.append(
                    pltpu.make_async_copy(paired.at[s, pair], cots.at[pair, s], own_sems.at[1 + CH + pair])
                )
                keeps[-1].start()
        if step == 0:
            row = lax.broadcasted_iota(jnp.int32, (2 * TOK, TOK), 0)
            column_of = lax.broadcasted_iota(jnp.int32, (2 * TOK, TOK), 1)
            block[...] = jnp.where(lax.rem(row, CP) == lax.rem(column_of, CP), 0.0, -1e30)
            cot[:, pl.ds(512, 128)] = jnp.zeros((TOK, 128), BF16)
            for keep in keeps:
                keep.wait()

    weight.collect(between)
    feed(FEEDS[7], 90)

    def forward(ch):
        came_all(send_x, ch)

        @pl.when(lax.rem(ch, 2) == 0)
        def _():
            came_all(send_c, lax.div(ch, 2))

        normalise(ch, tokens, cots, shift, scale, normed, cot)
        attention(ch, w, proj, gproj, normed, cot, block)

    def backward(ch):
        grad_normed(ch, w, gproj, gnorm)
        loop(0, SEQ // GROUP, lambda g: grad_tokens(ch, g, tokens, away, scale, gnorm))

    def early(ch):
        forward(ch)

        @pl.when(ch < 2)
        def _():
            backward(ch)
            keep_back(ch).start()

        @pl.when(ch == 1)
        def _():
            weight_partial(0, 2, normed, gproj, gw)

    loop(0, 3, early)
    weight_partial(2, 1, normed, gproj, gw)
    sent_all(send_x, 3)
    counts, started = iter(RETURNS), [0]

    def beside():
        first = started[0]
        started[0] = min(first + next(counts), 60)
        give_back(first, started[0])

    beside()
    forward(3)
    beside()
    weight_partial(3, 1, normed, gproj, gw)
    beside()
    total.begin(beside)

    def last_chunk():
        for ch in (2, 3):
            backward(ch)
            keep_back(ch).start()

    def returned(ch):
        for i in range(1, SEQ):
            send_back(ch, i).wait()
        keep_back(ch).wait()

    def settle():
        weight.finish()
        for pair in range(CH // 2):
            sent_all(send_c, pair)
        for ch in range(CH - 1):
            sent_all(send_x, ch)
        total.finish()
        for ch in range(CH - 1):
            returned(ch)

    total.sum_up(beside, last_chunk, settle)
    gout[...] = narrow([jnp.concatenate([tiles[5 * i + t].astype(F32) for t in range(5)], axis=1) for i in range(3)]).astype(
        BF16
    )
    returned(CH - 1)


FEEDS = (0, 8, 14, 20, 26, 38, 46, 52)
RETURNS = (10, 6, 6) + (0,) * 16 + (6, 6, 3, 2, 3, 3, 60)


def fused(x, cot, shift, scale, w):
    vm, hbm = pl.BlockSpec(memory_space=pltpu.VMEM), pl.BlockSpec(memory_space=pl.ANY)
    dma = pltpu.SemaphoreType.DMA
    return pl.pallas_call(
        kernel,
        out_shape=(jax.ShapeDtypeStruct(x.shape, BF16), jax.ShapeDtypeStruct((ROWS, 3 * INNER), BF16)),
        in_specs=[hbm, hbm, vm, vm, hbm],
        out_specs=(hbm, vm),
        scratch_shapes=[
            pltpu.VMEM((ROWS, 3 * INNER), BF16),
            pltpu.VMEM((INNER, PATCH), BF16),
            pltpu.VMEM((SEQ, CH // 2, CP, 2 * INNER), BF16),
            pltpu.VMEM((NQ, ROWS, 128), BF16),
            pltpu.VMEM((NQ, ROWS, 128), BF16),
            pltpu.VMEM((CH, SEQ, CP, D), BF16),
            pltpu.VMEM((CH // 2, SEQ, CP, 2 * INNER), BF16),
            pltpu.VMEM((CH, SEQ, CP, D), BF16),
            pltpu.VMEM((3, TOK, WIDE), BF16),
            pltpu.VMEM((3, CH * TOK, WIDE), BF16),
            pltpu.VMEM((CH * TOK, D), BF16),
            pltpu.VMEM((TOK, WIDE), BF16),
            pltpu.VMEM((TOK, D), F32),
            pltpu.VMEM((2 * TOK, TOK), F32),
            pltpu.VMEM((3, D, WIDE), BF16),
            pltpu.VMEM((3, D, WIDE), F32),
            pltpu.VMEM((2, 4, ROWS, 128), BF16),
            pltpu.VMEM((4, 4, 2, 4, ROWS, 128), BF16),
            pltpu.VMEM((4, 4, 2, 4, ROWS, 128), BF16),
            pltpu.VMEM((4, 4, 2, 4, ROWS, 128), BF16),
            pltpu.VMEM((4, 4, 2, 4, ROWS, 128), BF16),
            pltpu.VMEM((4, 4, 2, 4, ROWS, 128), BF16),
            pltpu.VMEM((2, 2, 4, 2, ROWS, 128), BF16),
            pltpu.VMEM((2, 2, 4, 4, ROWS, 128), BF16),
            pltpu.VMEM((2, 2, 2, ROWS, 128), BF16),
            pltpu.VMEM((2, 2, 4, ROWS, 128), BF16),
            pltpu.VMEM((3, 2, ROWS, 128), BF16),
            pltpu.VMEM((3, ROWS, 128), BF16),
        ]
        + [dma((CH, SEQ - 1))] * 2
        + [dma((CH // 2, SEQ - 1))] * 2
        + [dma((CH, SEQ - 1))] * 2
        + [
            dma((1 + 2 * CH,)),
            dma((4,)),
            dma((4,)),
            dma((2, 4, 2)),
            dma((2, 4, 2)),
            dma((2, 7)),
            dma((2, 7)),
            dma((2, 4)),
            dma((2, 4)),
            dma((2, 6, 2)),
            dma((2, 6, 2)),
            dma((6,)),
            dma((6,)),
            dma((NXY - 1,)),
            dma((NXY - 1,)),
        ],
        compiler_params=pltpu.CompilerParams(
            collective_id=0, has_side_effects=True, vmem_limit_bytes=60 * 1024 * 1024
        ),
        name="temporal_backward",
    )(x, cot, shift, scale, w)


def body(frames, shift_table, scale_table, grad_attended, w_qkv):
    x = frames.reshape(SEQ * CH, CP, D)
    cot = grad_attended[0, 0].T
    grad_tokens, grad_weight = fused(x, cot, shift_table, scale_table, w_qkv)
    return grad_tokens.reshape(frames.shape), grad_weight


def solution(mesh):
    placed = (
        P("dp", "seq", None, None),
        P("dp", None),
        P("dp", None),
        P("dp", "seq", None, None),
        P("seq", None),
    )
    return jax.shard_map(
        body,
        mesh=mesh,
        in_specs=placed,
        out_specs=(P("dp", "seq", None, None), P("seq", None)),
        check_vma=False,
    )
```
